128 devices in a mesh: grp: 2 (over y_hi), row: 8 (over x, core), col: 8 (over y_lo, z).
Axes of the slice: x: 4, y: 4 (y_hi: 2, y_lo: 2; y = y_hi * 2 + y_lo), z: 4, core: 2. Of those that a mesh axis runs over, the one named last changes fastest.
Arguments:
- child_update: bfloat16 [2, 7168, 1024], P('grp', ('row', 'col'))
- child_pivot: float32 [2, 1024, 1024], P('grp'), as said below
- child_map: int32 [2, 14], replicated, may hold values from 0 to 31, as said below
- parent_front: bfloat16 [16384, 16384], P('row', ('grp', 'col')), as said below
Outputs:
- front_out: float32 [16384, 16384], P('row', ('grp', 'col'))
The draws below stay inside these ranges and needn't reach their ends.
Inputs may be any that keep to these rules, and one draw needn't show every extreme that they name: `child_map`: each row is strictly increasing, starts at 0 and ends at 31. `child_pivot`: each child's block is symmetric positive definite. `parent_front`: exactly symmetric; the parent front minus the two children's updates is positive definite.
All inputs are finite; a program needn't handle non-finite values.
Results may differ from the reference program's by a relative error of at most 0.0043.
Values may be sent and summed in bfloat16 or wider, within the bound.
A program may use at most 256 MiB of HBM per device.

```python
import jax
import jax.numpy as jnp
from jax import lax

TB = 512
CT = 16
PT = 32


def shared_maps(key):
    base_key = jax.random.fold_in(key, 101)
    listed = []
    for child_index in range(2):
        shuffled = jax.random.permutation(jax.random.fold_in(base_key, child_index), PT - 2)
        chosen = jnp.sort(shuffled[:CT - 4]).astype(jnp.int32) + 1
        first_tile = jnp.zeros((1,), jnp.int32)
        last_tile = jnp.full((1,), PT - 1, jnp.int32)
        listed.append(jnp.concatenate([first_tile, chosen, last_tile]))
    return jnp.stack(listed)


def shared_factors(key):
    base_key = jax.random.fold_in(key, 202)
    width = 2 * TB
    update_rows = (CT - 2) * TB
    first_key = jax.random.fold_in(base_key, 0)
    second_key = jax.random.fold_in(base_key, 1)
    fourth_key = jax.random.fold_in(base_key, 3)
    coupling = jax.random.normal(first_key, (2, update_rows, width), jnp.float32) * width ** (-0.5)
    lower_part = jnp.tril(jax.random.normal(second_key, (2, width, width), jnp.float32)) * (0.5 * width ** (-0.5))
    diagonal_part = 1.0 + jax.random.uniform(fourth_key, (2, width), jnp.float32)
    pivot_root = lower_part + diagonal_part[:, :, None] * jnp.eye(width, dtype=jnp.float32)[None]
    return (coupling, pivot_root)


def draw_child_pivot(key, part):
    own_key = jax.random.fold_in(key, 3)
    coupling, pivot_root = shared_factors(key)
    width = 2 * TB
    product = jnp.einsum('gij,gkj->gik', pivot_root, pivot_root, precision=lax.Precision.HIGHEST)
    product = 0.5 * (product + jnp.swapaxes(product, 1, 2))
    extra = 0.2 * jax.random.uniform(own_key, (2, width), jnp.float32)
    return product + extra[:, :, None] * jnp.eye(width, dtype=jnp.float32)[None]


def draw_child_update(key, part):
    coupling, pivot_root = shared_factors(key)
    return jnp.einsum('gri,gki->grk', coupling, pivot_root, precision=lax.Precision.HIGHEST).astype(jnp.bfloat16)


def draw_parent_front(key, part):
    own_key = jax.random.fold_in(key, 5)
    coupling, pivot_root = shared_factors(key)
    tile_maps = shared_maps(key)
    order = PT * TB
    width = 2 * TB
    total = jnp.zeros((order, order), jnp.float32)
    for child_index in range(2):
        spread = jnp.zeros((PT, TB, width), jnp.float32).at[tile_maps[child_index]].set(coupling[child_index].reshape(CT - 2, TB, width))
        spread = spread.reshape(order, width)
        total = total + jnp.dot(spread, spread.T, precision=lax.Precision.HIGHEST)
    mix_key, diag_key = jax.random.split(own_key, 2)
    mixing = jax.random.normal(mix_key, (order, TB), jnp.float32)
    total = total + jnp.dot(mixing, mixing.T, precision=lax.Precision.HIGHEST) / TB
    total = 0.5 * (total + total.T)
    return (total + jnp.diag(1.0 + jax.random.uniform(diag_key, (order,), jnp.float32))).astype(jnp.bfloat16)


def draw_child_map(key, part):
    return shared_maps(key)


def setup_inputs(seed: int = 0) -> dict:
    seeds = jax.random.split(jax.random.key(seed), 5)
    child_update = draw_child_update(jax.random.fold_in(seeds[4], 71), 0)
    child_pivot = draw_child_pivot(jax.random.fold_in(seeds[4], 71), 0)
    child_map = draw_child_map(jax.random.fold_in(seeds[4], 71), 0)
    parent_front = draw_parent_front(jax.random.fold_in(seeds[4], 71), 0)
    return {"child_update": child_update, "child_pivot": child_pivot, "child_map": child_map, "parent_front": parent_front}


def right_solve(factor, right_side):
    return lax.linalg.triangular_solve(factor, right_side, left_side=False, lower=True, transpose_a=True)

def reference(child_update, child_pivot, child_map, parent_front):
    width = child_pivot.shape[-1]
    order = parent_front.shape[0]
    assembled = parent_front.astype(jnp.float32)
    for child_index in range(2):
        child_factor = jnp.linalg.cholesky(child_pivot[child_index])
        child_panel = right_solve(child_factor, child_update[child_index].astype(jnp.float32)).astype(jnp.bfloat16)
        spread = jnp.zeros((PT, TB, width), jnp.bfloat16).at[child_map[child_index]].set(child_panel.reshape(-1, TB, width))
        spread = spread.reshape(order, width)
        assembled = assembled - jnp.dot(spread.astype(jnp.float32), spread.T.astype(jnp.float32), preferred_element_type=jnp.float32)
    pivot_factor = jnp.linalg.cholesky(assembled[:width, :width])
    panel_factor = right_solve(pivot_factor, assembled[width:, :width])
    panel_rounded = panel_factor.astype(jnp.bfloat16)
    schur = assembled[width:, width:] - jnp.dot(panel_rounded.astype(jnp.float32), panel_rounded.T.astype(jnp.float32), preferred_element_type=jnp.float32)
    upper_rows = jnp.concatenate([pivot_factor, jnp.zeros((width, order - width), jnp.float32)], axis=1)
    lower_rows = jnp.concatenate([panel_factor, schur], axis=1)
    return jnp.concatenate([upper_rows, lower_rows], axis=0)
```

```python
import functools

import jax
import jax.numpy as jnp
from jax import lax
from jax.experimental import pallas as pl
from jax.experimental.pallas import tpu as pltpu
from jax.sharding import PartitionSpec as P

TB = 512
F32 = jnp.float32
BF16 = jnp.bfloat16
NB = 128
SUBS = 8
VM = pltpu.VMEM
NT = (((1,), (1,)), ((), ()))
NN = (((1,), (0,)), ((), ()))


CUT = 256


def dot16(a, b, dims=NN):
    return lax.dot_general(a, b, dims, preferred_element_type=F32)


def split(x):
    hi = x.astype(BF16)
    return hi, (x - hi.astype(F32)).astype(BF16)


def dot_nt(a, b):
    return lax.dot_general(
        a, b, NT, precision=lax.Precision.HIGHEST, preferred_element_type=F32
    )


def sum_products(x, y):
    terms = [a * b for a, b in zip(x, y)]
    while len(terms) > 1:
        paired = [terms[i] + terms[i + 1] for i in range(0, len(terms) - 1, 2)]
        terms = paired + ([terms[-1]] if len(terms) % 2 else [])
    return terms[0]


class Block:
    def __init__(self, p):
        self.n = len(p)
        if self.n == 2:
            a, b, c = p[0][0], p[1][0], p[1][1]
            det = a * c - b * b
            q = 1.0 / det
            self.entries = (a, b, det)
            self.inverse = (c * q, -b * q, a * q)
            return
        h = self.n // 2
        self.first = Block([row[:h] for row in p[:h]])
        below = [[p[h + x][y] for y in range(h)] for x in range(h)]
        self.gain = [self.first.solve(row) for row in below]
        self.second = Block(
            [
                [p[h + x][h + y] - sum_products(self.gain[x], below[y]) for y in range(x + 1)]
                for x in range(h)
            ]
        )

    def reduce(self, rows):
        h = self.n // 2
        return [rows[h + x] - sum_products(self.gain[x], rows[:h]) for x in range(h)]

    def solve(self, rows):
        if self.n == 2:
            i00, i01, i11 = self.inverse
            return [i00 * rows[0] + i01 * rows[1], i01 * rows[0] + i11 * rows[1]]
        h = self.n // 2
        top = self.first.solve(rows[:h])
        bottom = self.second.solve(self.reduce(rows))
        top = [
            top[y] - sum_products([self.gain[x][y] for x in range(h)], bottom) for y in range(h)
        ]
        return top + bottom

    def half_solve(self, rows):
        if self.n == 2:
            a, b, det = self.entries
            scale = lax.rsqrt(a)
            inv_a = scale * scale
            return [
                rows[0] * scale,
                (rows[1] - (b * inv_a) * rows[0]) * lax.rsqrt(det * inv_a),
            ]
        return self.first.half_solve(rows[: self.n // 2]) + self.second.half_solve(
            self.reduce(rows)
        )


def factor_diagonal(tiles):
    tiles = list(tiles)
    lanes = lax.broadcasted_iota(jnp.int32, (8, 128), 1)
    subs = lax.broadcasted_iota(jnp.int32, (8, 128), 0)
    upper, inverse = [], []
    for v in range(16):
        j = 8 * v
        inside = (lanes >= j) & (lanes < j + SUBS)
        cols = [
            {i: jnp.broadcast_to(tiles[i][:, j + k : j + k + 1], (8, 128)) for i in range(v, 16)}
            for k in range(SUBS)
        ]
        rows = [jnp.broadcast_to(tiles[v][k : k + 1, :], (8, 128)) for k in range(SUBS)]
        pivots = [
            [jnp.broadcast_to(cols[l][v][k : k + 1, :], (8, 128)) for l in range(k + 1)]
            for k in range(SUBS)
        ]
        unit_rows = [
            jnp.where(inside, jnp.where(lanes == j + k, F32(1), F32(0)), rows[k])
            for k in range(SUBS)
        ]
        block = Block(pivots)
        solved = block.solve(unit_rows)
        up, inv = block.half_solve(rows), block.half_solve(unit_rows)
        up_tile, inv_tile = up[0], inv[0]
        for k in range(1, SUBS):
            up_tile = jnp.where(subs == k, up[k], up_tile)
            inv_tile = jnp.where(subs == k, inv[k], inv_tile)
        upper.append(jnp.where(lanes >= subs + j, up_tile, F32(0)))
        inverse.append(jnp.where(lanes <= subs + j, inv_tile, F32(0)))
        for i in range(v + 1, 16):
            tiles[i] = jnp.where(inside, F32(0), tiles[i]) - sum_products(
                [cols[k][i] for k in range(SUBS)], solved
            )
    return upper, inverse


AXES = ("x", "y", "z")
CUTS = ((0, 384), (384, 384), (768, 256))
ORDERS = (("y", "z", "x"), ("z", "x", "y"), ("x", "y", "z"))
LINKS = 128


class Mover:
    def __init__(self, send_sems, recv_sems):
        self.send_sems, self.recv_sems = send_sems, recv_sems
        row, col, grp = lax.axis_index("row"), lax.axis_index("col"), lax.axis_index("grp")
        self.row = row
        self.core = lax.rem(row, 2)
        self.at = {"x": row // 2, "y": grp * 2 + col // 4, "z": lax.rem(col, 4)}
        self.count = 0
        self.sent = []

    def device(self, axis, place):
        if axis == "x":
            return {"row": place * 2 + self.core}
        if axis == "y":
            return {"grp": place // 2, "col": lax.rem(place, 2) * 4 + self.at["z"]}
        return {"col": (self.at["y"] - self.at["y"] // 2 * 2) * 4 + place}

    def sibling(self):
        return {"row": self.row + 1 - 2 * self.core}

    def shifted(self, axis, by):
        return lax.rem(self.at[axis] + (by + 4), 4)

    def greet(self):
        barrier = pltpu.get_barrier_semaphore()
        others = [self.sibling()]
        for axis in AXES:
            others += [self.device(axis, self.shifted(axis, by)) for by in (1, 2, 3)]
        for other in others:
            pl.semaphore_signal(
                barrier, inc=1, device_id=other, device_id_type=pl.DeviceIdType.MESH
            )
        pl.semaphore_wait(barrier, len(others))

    def make(self, src, dst, device, send=True):
        i = self.count
        self.count += 1
        copy = pltpu.make_async_remote_copy(
            src_ref=src,
            dst_ref=dst,
            send_sem=self.send_sems.at[i],
            recv_sem=self.recv_sems.at[i],
            device_id=device,
            device_id_type=pl.DeviceIdType.MESH,
        )
        return copy

    def ring(self, axis, region, when=None):
        here = self.at[axis]
        ahead, behind = self.shifted(axis, 1), self.shifted(axis, -1)
        toward = lax.rem(here + 1 + 2 * self.core, 4)
        away = lax.rem(here + 3 - 2 * self.core, 4)
        plus = self.make(region(here), region(here), self.device(axis, ahead))
        minus = self.make(region(here), region(here), self.device(axis, behind))
        passed = self.make(region(away), region(away), self.device(axis, toward))
        self.sent += [(c, when) for c in (plus, minus, passed)]

        def first():
            plus.start()
            minus.start()

        def second():
            plus.wait_recv()
            minus.wait_recv()
            passed.start()

        def third():
            passed.wait_recv()

        return [guard(when, f) for f in (first, second, third)]

    def scatter(self, axis, source, target, when=None):
        here = self.at[axis]
        root, leaf = here == 0, here != 0
        if when is not None:
            root, leaf = root & when, leaf & when
        i = self.count
        self.count += 3
        recv = self.recv_sems.at[i]
        copies = []
        for k in (1, 2, 3):
            copies.append(
                pltpu.make_async_remote_copy(
                    src_ref=source(k),
                    dst_ref=target(k),
                    send_sem=self.send_sems.at[i + k - 1],
                    recv_sem=recv,
                    device_id=self.device(axis, k),
                    device_id_type=pl.DeviceIdType.MESH,
                )
            )
        self.sent += [(c, root) for c in copies]

        def first():
            for c in copies:
                c.start()

        def second():
            copies[0].wait_recv()

        return [guard(root, first), guard(leaf, second)]

    def push(self, region, when=None, taken=None):
        copy = self.make(region, region, self.sibling())
        self.sent.append((copy, when))
        return guard(when, copy.start), guard(taken, copy.wait_recv)

    def finish(self):
        for copy, when in self.sent:
            guard(when, copy.wait_send)()


def guard(when, f):
    if when is None:
        return f

    def guarded():
        pl.when(when)(f)

    return guarded


def merge(*steps):
    def run():
        for s in steps:
            s()

    return run


def rows_of(ref, start, count, cols=None):
    start = pl.multiple_of(start, 16)
    if cols is None:
        return ref.at[pl.ds(start, count)]
    return ref.at[pl.ds(start, count), pl.ds(*cols)]


def gather_program(
    raw, parent, g_ref, d_ref, st_ref, m_ref, u_ref, e_ref, lead, m_far, e_x, e_y, st_a, sems
):
    send_sems, recv_sems, local_sems = sems
    mv = Mover(send_sems, recv_sems)
    x, y, z, core = mv.at["x"], mv.at["y"], mv.at["z"], mv.core
    locals_made = []

    def local(src, dst, when=None):
        copy = pltpu.make_async_copy(src, dst, local_sems.at[len(locals_made)])
        locals_made.append(copy)
        return guard(when, copy.start), guard(when, copy.wait)

    def block(place, cut):
        gy = (place["y"] // 2, lax.rem(place["y"], 2)) if "y" in place else (slice(None),) * 2
        px = place.get("x", slice(None))
        pz = place.get("z", slice(None))
        return g_ref.at[gy[0], px, core, gy[1], pz, :, pl.ds(*cut)]

    own = local(raw, g_ref.at[y // 2, x, core, lax.rem(y, 2), z])
    a_lists = []
    for cut, order in zip(CUTS, ORDERS):
        place = dict(mv.at)
        steps = []
        for stage, axis in enumerate(order):
            ring = mv.ring(axis, lambda k, p=dict(place), a=axis: block({**p, a: k}, cut))
            if stage == 2:
                base = mv.push(block(place, cut))
                near = [mv.push(block({**place, axis: mv.shifted(axis, by)}, cut)) for by in (1, 3)]
                far = mv.push(block({**place, axis: mv.shifted(axis, 2)}, cut))
                ring[0] = merge(ring[0], base[0])
                ring[1] = merge(ring[1], near[0][0], near[1][0])
                ring[2] = merge(ring[2], far[0])
                ring.append(merge(base[1], near[0][1], near[1][1], far[1]))
            steps += ring
            del place[axis]
        a_lists.append(steps)

    lead_core = core == 0
    part_d = lambda k: rows_of(d_ref, k * 256, 256)
    d_root = local(parent.at[pl.ds(0, 256)], d_ref.at[pl.ds(0, 256)], lead_core & (x == 0))
    hand = mv.scatter("x", lambda k: rows_of(parent, k * 256, 256), part_d, lead_core)
    turn = mv.ring("x", part_d, lead_core)
    push = mv.push(d_ref, lead_core, core == 1)
    d_steps = [
        merge(d_root[0], hand[0]),
        merge(d_root[1], hand[1], turn[0]),
        turn[1],
        merge(turn[2], push[0]),
        push[1],
    ]

    e_row = x * 256 + y * 64 + z * 16
    cut_z = lambda k: rows_of(e_ref, x * 256 + y * 64 + k * 16, 16)
    cut_y = lambda k: rows_of(e_ref, x * 256 + k * 64, 64)
    cut_x = lambda k: rows_of(e_ref, k * 256, 256)
    on_x = lead_core & (y == 0) & (z == 0)
    on_y = lead_core & (z == 0)
    loc_x = local(parent.at[pl.ds(0, 256)], e_x, on_x & (x == 0))
    loc_y = local(e_x.at[pl.ds(0, 64)], e_y, on_y & (y == 0))
    loc_z = local(e_y.at[pl.ds(0, 16)], rows_of(e_ref, e_row, 16), on_y)
    hand_x = mv.scatter("x", lambda k: rows_of(parent, k * 256, 256), lambda k: e_x, on_x)
    hand_y = mv.scatter("y", lambda k: e_x.at[pl.ds(64 * k, 64)], lambda k: e_y, on_y)
    hand_z = mv.scatter("z", lambda k: e_y.at[pl.ds(16 * k, 16)], cut_z, lead_core)
    turn_z = mv.ring("z", cut_z, lead_core)
    turn_y = mv.ring("y", cut_y, lead_core)
    turn_x = mv.ring("x", cut_x, lead_core)
    push = mv.push(e_ref, lead_core, core == 1)
    e_steps = [
        merge(loc_x[0], hand_x[0]),
        merge(loc_x[1], hand_x[1], loc_y[0], hand_y[0]),
        merge(loc_y[1], hand_y[1], loc_z[0], hand_z[0]),
        merge(loc_z[1], hand_z[1], turn_z[0]),
        turn_z[1],
        merge(turn_z[2], turn_y[0]),
        turn_y[1],
        merge(turn_y[2], turn_x[0]),
        turn_x[1],
        merge(turn_x[2], push[0]),
        push[1],
    ]

    st_lists = []
    for i, ((a, b), cut) in enumerate(((("z", "y"), (0, 512)), (("y", "z"), (512, 512)))):
        wide = lambda k, cut=cut: rows_of(st_ref, k * 512, 512, cut)
        wide_source = lambda k, cut=cut: rows_of(parent, k * 512, 512, cut)
        fine = lambda k, a=a, cut=cut: rows_of(st_ref, mv.at[a] * 512 + k * 128, 128, cut)
        held = st_a.at[i]
        line = mv.at[b] == 0
        loc_a = local(wide_source(0), held, line & (mv.at[a] == 0))
        loc_b = local(held.at[pl.ds(0, 128)], fine(0), line)
        hand_a = mv.scatter(a, wide_source, lambda k: held, line)
        hand_b = mv.scatter(b, lambda k: held.at[pl.ds(k * 128, 128)], fine)
        turn_b = mv.ring(b, fine)
        turn_a = mv.ring(a, wide)
        st_lists.append(
            [
                merge(loc_a[0], hand_a[0]),
                merge(loc_a[1], hand_a[1], loc_b[0], hand_b[0]),
                merge(loc_b[1], hand_b[1], turn_b[0]),
                turn_b[1],
                merge(turn_b[2], turn_a[0]),
                turn_a[1],
                turn_a[2],
            ]
        )

    y_lo = lax.rem(y, 2)
    base = core * (2 * 4 * raw.shape[0])
    size = raw.shape[0]
    chunk_z = lambda k: rows_of(u_ref, base + (y_lo * 4 + k) * size, size)
    u_own = local(raw, chunk_z(z), x == 0)
    u_hand = mv.scatter("x", lambda k: raw, lambda k: chunk_z(z))
    u_turn = mv.ring("z", chunk_z)
    full = 8 * size
    rest = e_ref.shape[0] - full
    beside = {"col": (1 - y_lo) * 4 + z}
    half = rows_of(u_ref, y_lo * 4 * size, 4 * size)
    swap = mv.make(half, half, beside)
    mv.sent.append((swap, lead_core))
    tail = u_ref.at[pl.ds(full, rest)]
    slide = mv.make(tail, tail, beside)
    mv.sent.append((slide, (core == 1) & (y_lo == 0)))
    push_head = mv.push(u_ref.at[pl.ds(0, full)], lead_core, core == 1)
    push_tail = mv.push(tail, core == 1, lead_core)
    u_steps = [
        merge(u_own[0], u_hand[0]),
        merge(u_own[1], u_hand[1], u_turn[0]),
        u_turn[1],
        merge(
            u_turn[2],
            guard(lead_core, swap.start),
            guard((core == 1) & (y_lo == 0), slide.start),
        ),
        merge(
            guard(lead_core, swap.wait_recv),
            guard((core == 1) & (y_lo == 1), slide.wait_recv),
            push_head[0],
            push_tail[0],
        ),
        merge(push_head[1], push_tail[1]),
    ]

    def exchange(mine, theirs):
        start = core * 512 + x * 128 + z * 32
        across = mv.make(mine(start, 32), theirs(start, 32), mv.device("y", mv.shifted("y", 2)))
        mv.sent.append((across, None))
        turn_z = mv.ring("z", lambda k: theirs(core * 512 + x * 128 + k * 32, 32))
        turn_x = mv.ring("x", lambda k: theirs(core * 512 + k * 128, 128))
        push = mv.push(theirs(core * 512, 512))
        return [
            across.start,
            merge(across.wait_recv, turn_z[0]),
            turn_z[1],
            merge(turn_z[2], turn_x[0]),
            turn_x[1],
            merge(turn_x[2], push[0]),
            push[1],
        ]

    def part(ref, *lead_index):
        return lambda start, n: ref.at[lead_index + (pl.ds(pl.multiple_of(start, 16), n),)]

    x_steps = exchange(part(lead, 0), part(lead, 1))
    m_steps = exchange(part(m_ref, slice(None)), part(m_far, slice(None)))
    assert mv.count <= LINKS
    a, st = [[merge(*s) for s in zip(*lists)] for lists in (a_lists, st_lists)]
    d, e, u, m = d_steps, e_steps, u_steps, m_steps
    early = [
        merge(mv.greet, own[0], u[0], e[0], own[1], a[0]),
        merge(u[1], e[1]),
        a[1],
        merge(u[2], e[2]),
        merge(u[3], a[2], a[3]),
        e[3],
        merge(u[4], e[4]),
        e[5],
        merge(a[4], e[6]),
        merge(e[7], d[0]),
        merge(u[5], e[8]),
        merge(a[5], a[6], e[9]),
        merge(e[10], d[1]),
        d[2],
        st[0],
    ]
    late = [
        merge(m[0], d[3]),
        a[7],
        merge(m[1], st[1]),
        d[4],
        merge(m[2], st[2]),
        a[8],
        merge(m[3], st[3]),
        m[4],
        st[4],
        m[5],
        st[5],
        m[6],
        merge(st[6], a[9]),
    ]
    return mv, early, x_steps, late


def factor_loop(w, inv_s, up_s, l_ref, ticks):
    width = w.shape[0]
    steps = width // NB
    if l_ref is not None:
        l_ref[...] = jnp.zeros_like(l_ref)

    def step(k, _):
        o = pl.multiple_of(k * NB, NB)
        here = pl.ds(o, NB)
        for i in range(0, len(ticks), 2):
            pl.when(k == i // 2)(ticks[i])
        groups = [w[pl.ds(pl.multiple_of(o + 8 * i, 8), 8), here] for i in range(NB // 8)]
        up, inv = factor_diagonal(groups)
        for i in range(NB // 8):
            inv_s[8 * i : 8 * i + 8, :] = inv[i]
            up_s[8 * i : 8 * i + 8, :] = up[i]
        inverse = inv_s[...]
        w[:, here] = dot_nt(w[:, here], inverse)
        w[here, here] = inverse.T
        if l_ref is not None:
            l_ref[here, here] = up_s[...].T

            def keep(j, _):
                below = pl.ds(pl.multiple_of(j * NB, NB), NB)
                l_ref[below, here] = w[below, here]
                return 0

            lax.fori_loop(k + 1, steps, keep, 0)
        for i in range(1, len(ticks), 2):
            pl.when(k == i // 2)(ticks[i])

        def update(j, _):
            there = pl.ds(pl.multiple_of(j * NB, NB), NB)
            w[here, there] = jnp.zeros((NB, NB), F32)
            w[:, there] -= dot_nt(w[:, here], w[there, here])
            return 0

        lax.fori_loop(k + 1, steps, update, 0)
        return 0

    lax.fori_loop(0, steps, step, 0)


def split_upper(w, m_ref):
    width = w.shape[0]
    for n in range(width // NB):
        cut = slice(n * NB, (n + 1) * NB)
        end = (n + 1) * NB
        hi, lo = split(w[:end, cut])
        m_ref[0, :end, cut] = hi
        m_ref[1, :end, cut] = lo
        if end < width:
            m_ref[:, end:, cut] = jnp.zeros((2, width - end, NB), BF16)


def front_kernel(
    a_ref, keep_ref, raw, parent,
    m_ref, m_pivot, l_ref, g_ref, d_ref, st_ref, lead_out, far_out,
    w, inv_s, up_s, u_ref, e_ref, lead, m_far, e_x, e_y, st_a, send_sems, recv_sems, local_sems,
):
    width = a_ref.shape[0]
    mv, early, swap, late = gather_program(
        raw, parent, g_ref, d_ref, st_ref, m_ref, u_ref, e_ref, lead, m_far, e_x, e_y, st_a,
        (send_sems, recv_sems, local_sems),
    )
    w[...] = a_ref[...]
    factor_loop(w, inv_s, up_s, None, early)
    split_upper(w, m_ref)
    for n in range(width // CUT):
        end = (n + 1) * CUT
        cut = slice(n * CUT, end)
        rows = u_ref[:width, :end]
        both = dot16(rows, m_ref[0, :end, cut]) + dot16(rows, m_ref[1, :end, cut])
        lead[0, :, cut] = (both * keep_ref[:, :1]).astype(BF16)
    for step in swap:
        step()
    lead_copy = pltpu.make_async_copy(lead, lead_out, local_sems.at[14])
    far_copy = pltpu.make_async_copy(m_far, far_out, local_sems.at[15])
    lead_copy.start()
    for n in range(width // CUT):
        start = n * CUT
        cut = slice(start, start + CUT)
        total = e_ref[start:, cut].astype(F32)
        for i in range(2):
            total -= dot16(lead[i, start:, :], lead[i, cut, :], NT)
        w[start:, cut] = total
    factor_loop(w, inv_s, up_s, l_ref, late)
    far_copy.start()
    split_upper(w, m_pivot)
    mv.finish()
    lead_copy.wait()
    far_copy.wait()


def front(block, keep, raw, parent):
    width = block.shape[0]
    chunk = raw.shape[0]
    hbm = pl.BlockSpec(memory_space=pl.ANY)
    vmem = pl.BlockSpec(memory_space=VM)
    pair = jax.ShapeDtypeStruct((2, width, width), BF16)
    return pl.pallas_call(
        front_kernel,
        out_shape=[
            pair,
            pair,
            jax.ShapeDtypeStruct((width, width), F32),
            jax.ShapeDtypeStruct((2, 4, 2, 2, 4, chunk, width), BF16),
            jax.ShapeDtypeStruct((width, width), BF16),
            jax.ShapeDtypeStruct(parent.shape, BF16),
            pair,
            pair,
        ],
        in_specs=[vmem, vmem, hbm, hbm],
        out_specs=[vmem, vmem, vmem, hbm, hbm, hbm, hbm, hbm],
        scratch_shapes=[
            VM((width, width), F32),
            VM((NB, NB), F32),
            VM((NB, NB), F32),
            VM((16 * chunk, width), BF16),
            VM((width, width), BF16),
            VM((2, width, width), BF16),
            VM((2, width, width), BF16),
            VM((256, width), BF16),
            VM((64, width), BF16),
            VM((2, 512, 512), BF16),
            pltpu.SemaphoreType.DMA((LINKS,)),
            pltpu.SemaphoreType.DMA((LINKS,)),
            pltpu.SemaphoreType.DMA((16,)),
        ],
        compiler_params=pltpu.CompilerParams(
            vmem_limit_bytes=52 * 2**20, collective_id=0, has_side_effects=True
        ),
        cost_estimate=pl.CostEstimate(
            flops=120_000_000_000, bytes_accessed=16 * width * width, transcendentals=0
        ),
        name="front",
    )(block, keep, raw, parent)


def chunk_span(chunk):
    return -(-(TB + chunk - 16) // chunk)


def spread_kernel(
    chunk, tile_ref, have_ref, grp_ref, gathered, own_ref, far_ref, lead_ref, d_ref, st_ref,
    s_ref, b_ref, buf, sem,
):
    t, g = pl.program_id(0), pl.program_id(1)
    width = lead_ref.shape[1]
    chunks = gathered.shape[1]
    across = 2
    span = chunk_span(chunk)
    slot = lax.rem(t * 2 + g, 2)

    def copies(t, g, slot):
        row = tile_ref[g * 6 + t] * TB
        first = row // chunk
        out = []
        for i in range(span):
            c = jnp.minimum(first + i, chunks - 1)
            out.append(
                pltpu.make_async_copy(
                    gathered.at[g ^ grp_ref[0], c],
                    buf.at[slot, pl.ds(i * chunk, chunk)],
                    sem.at[slot, i],
                )
            )
        return out

    @pl.when((t == 0) & (g == 0))
    def _():
        for c in copies(t, g, slot):
            c.start()

    nxt = t * 2 + g + 1

    @pl.when(nxt < 12)
    def _():
        for c in copies(nxt // 2, lax.rem(nxt, 2), 1 - slot):
            c.start()

    for c in copies(t, g, slot):
        c.wait()

    @pl.when((g == 0) & (t < across))
    def _():
        b_ref[...] = d_ref[...].astype(F32).T

    @pl.when((g == 0) & (t >= across))
    def _():
        b_ref[...] = st_ref[...].astype(F32)

    have = have_ref[g * 6 + t] != 0

    @pl.when(jnp.logical_not(have))
    def _():
        s_ref[...] = jnp.zeros_like(s_ref)

    row = tile_ref[g * 6 + t] * TB
    rows = pl.ds(pl.multiple_of(lax.rem(row, chunk), 16), TB)

    def fill(m_ref):
        for n in range(width // CUT):
            end = (n + 1) * CUT
            cut = slice(n * CUT, end)
            held = buf[slot, rows, :end]
            part = dot16(held, m_ref[0, :end, cut]) + dot16(held, m_ref[1, :end, cut])
            s_ref[:, cut] = part.astype(BF16)
        b_ref[...] -= dot16(s_ref[...], lead_ref[g], NT)

    pl.when(have & (g == 0))(lambda: fill(own_ref))
    pl.when(have & (g == 1))(lambda: fill(far_ref))


def spread(tiles, have, grp, gathered, m_own, m_far, lead_both, column_panel, stripe):
    chunk = gathered.shape[2]
    width = lead_both.shape[-1]
    across = column_panel.shape[1] // TB
    rows = column_panel.shape[1] + stripe.shape[0]
    vmem = pl.BlockSpec(memory_space=VM)
    return pl.pallas_call(
        functools.partial(spread_kernel, chunk),
        grid_spec=pltpu.PrefetchScalarGridSpec(
            num_scalar_prefetch=3,
            grid=(rows // TB, 2),
            in_specs=[
                pl.BlockSpec(memory_space=pl.ANY),
                vmem,
                vmem,
                vmem,
                pl.BlockSpec((width, TB), lambda t, g, *_: (0, jnp.minimum(t, across - 1))),
                pl.BlockSpec((TB, width), lambda t, g, *_: (jnp.maximum(t - across, 0), 0)),
            ],
            out_specs=[
                pl.BlockSpec((TB, width), lambda t, g, *_: (t, g)),
                pl.BlockSpec((TB, width), lambda t, g, *_: (t, 0)),
            ],
            scratch_shapes=[
                VM((2, chunk_span(chunk) * chunk, width), BF16),
                pltpu.SemaphoreType.DMA((2, chunk_span(chunk))),
            ],
        ),
        out_shape=[
            jax.ShapeDtypeStruct((rows, 2 * width), BF16),
            jax.ShapeDtypeStruct((rows, width), F32),
        ],
        compiler_params=pltpu.CompilerParams(vmem_limit_bytes=52 * 2**20),
        cost_estimate=pl.CostEstimate(
            flops=35_000_000_000, bytes_accessed=40 * 2**20, transcendentals=0
        ),
        name="spread",
    )(tiles, have, grp, gathered, m_own, m_far, lead_both, column_panel, stripe)


def trailing_kernel(across, flag_ref, s_ref, b_ref, m_ref, l_ref, parent_ref, out_ref, s_keep, f_keep):
    t = pl.program_id(0)
    width = b_ref.shape[1]
    b_hi, b_lo = split(b_ref[...])
    panels = []
    for n in range(width // CUT):
        end = (n + 1) * CUT
        cut = slice(n * CUT, end)
        hi, lo = m_ref[0, :end, cut], m_ref[1, :end, cut]
        panels.append(
            dot16(b_hi[:, :end], hi) + dot16(b_hi[:, :end], lo) + dot16(b_lo[:, :end], hi)
        )

    @pl.when(t < across)
    def _():
        here = pl.ds(pl.multiple_of(t * TB, TB), TB)
        s_keep[here, :] = s_ref[...]
        for n in range(width // CUT):
            f_keep[here, n * CUT : (n + 1) * CUT] = panels[n].astype(BF16)

    @pl.when(t >= across)
    def _():
        first = flag_ref[0] != 0
        pivot = (flag_ref[1] != 0) & (t < across + width // TB)

        @pl.when(first & pivot)
        def _():
            out_ref[...] = l_ref[...]

        @pl.when(first & jnp.logical_not(pivot))
        def _():
            for n in range(width // CUT):
                out_ref[:, n * CUT : (n + 1) * CUT] = panels[n]

        @pl.when(jnp.logical_not(first) & pivot)
        def _():
            out_ref[...] = jnp.zeros_like(out_ref)

        @pl.when(jnp.logical_not(first) & jnp.logical_not(pivot))
        def _():
            f = jnp.concatenate([p.astype(BF16) for p in panels], axis=1)
            out_ref[...] = parent_ref[...].astype(F32) - (
                dot16(s_ref[...], s_keep[...], NT) + dot16(f, f_keep[...], NT)
            )


def trailing(flags, s_all, b_all, m_pivot, pivot_factor, parent):
    width = b_all.shape[1]
    cols = parent.shape[1]
    across = cols // TB
    tiles = parent.shape[0] // TB
    lead = width // TB
    return pl.pallas_call(
        functools.partial(trailing_kernel, across),
        grid_spec=pltpu.PrefetchScalarGridSpec(
            num_scalar_prefetch=1,
            grid=(across + tiles,),
            in_specs=[
                pl.BlockSpec((TB, 2 * width), lambda t, *_: (t, 0)),
                pl.BlockSpec((TB, width), lambda t, *_: (t, 0)),
                pl.BlockSpec(memory_space=VM),
                pl.BlockSpec((TB, width), lambda t, *_: (jnp.clip(t - across, 0, lead - 1), 0)),
                pl.BlockSpec((TB, cols), lambda t, *_: (jnp.maximum(t - across, 0), 0)),
            ],
            out_specs=pl.BlockSpec((TB, cols), lambda t, *_: (jnp.maximum(t - across, 0), 0)),
            scratch_shapes=[VM((cols, 2 * width), BF16), VM((cols, width), BF16)],
        ),
        out_shape=jax.ShapeDtypeStruct(parent.shape, F32),
        compiler_params=pltpu.CompilerParams(vmem_limit_bytes=56 * 2**20),
        cost_estimate=pl.CostEstimate(flops=35_000_000_000, bytes_accessed=40 * 2**20, transcendentals=0),
        name="trailing",
    )(flags, s_all, b_all, m_pivot, pivot_factor, parent)


def locate(tile_map, parent_tiles):
    matches = tile_map[:, None] == jnp.arange(parent_tiles, dtype=jnp.int32)[None, :]
    positions = jnp.arange(tile_map.shape[0], dtype=jnp.int32)[:, None]
    return jnp.sum(jnp.where(matches, positions, 0), axis=0), jnp.any(matches, axis=0)


def per_device(child_update, child_pivot, child_map, parent_front):
    width = child_pivot.shape[-1]
    stripe_rows, block_cols = parent_front.shape
    row_tiles = stripe_rows // TB
    col_tiles = block_cols // TB
    parent_tiles = row_tiles * lax.axis_size("row")
    row = lax.axis_index("row")
    block = lax.axis_index(("grp", "col"))
    raw = child_update[0]
    chunk = raw.shape[0]

    grp = lax.axis_index("grp")
    own_map = jnp.where(grp == 0, child_map, child_map[::-1])
    lead_tiles = jnp.arange(width // TB, dtype=jnp.int32)
    keep = (own_map[0, : width // TB] == lead_tiles).astype(F32)
    keep = jnp.broadcast_to(jnp.repeat(keep, TB)[:, None], (width, 128))
    m_own, m_pivot, pivot_factor, gathered, column_panel, stripe, lead_both, m_far = front(
        child_pivot[0], keep, raw, parent_front
    )
    gathered = gathered.reshape(2, -1, chunk, width)

    wanted_tiles = jnp.concatenate(
        [
            block * col_tiles + jnp.arange(col_tiles, dtype=jnp.int32),
            row * row_tiles + jnp.arange(row_tiles, dtype=jnp.int32),
        ]
    )
    tiles, have = [], []
    for g in range(2):
        inverse, present = locate(own_map[g], parent_tiles)
        tiles.append(inverse[wanted_tiles])
        have.append(present[wanted_tiles].astype(jnp.int32))
    tiles, have = jnp.concatenate(tiles), jnp.concatenate(have)
    s_all, b_all = spread(
        tiles, have, grp[None], gathered, m_own, m_far, lead_both, column_panel, stripe
    )
    flags = jnp.stack([block == 0, row == 0]).astype(jnp.int32)
    return trailing(flags, s_all, b_all, m_pivot, pivot_factor, parent_front)


def solution(mesh):
    in_specs = (P("grp", ("row", "col"), None), P("grp", None, None), P(), P("row", ("grp", "col")))
    out_specs = P("row", ("grp", "col"))
    return jax.shard_map(
        per_device, mesh=mesh, in_specs=in_specs, out_specs=out_specs, check_vma=False
    )
```

```python
import functools

import jax
import jax.numpy as jnp
from jax import lax
from jax.experimental import pallas as pl
from jax.experimental.pallas import tpu as pltpu
from jax.sharding import PartitionSpec as P

TB = 512
F32 = jnp.float32
BF16 = jnp.bfloat16
NB = 128
SUBS = 8
VM = pltpu.VMEM
NT = (((1,), (1,)), ((), ()))
NN = (((1,), (0,)), ((), ()))


CUT = 256
WIDE = 512


def dot16(a, b, dims=NN):
    return lax.dot_general(a, b, dims, preferred_element_type=F32)


def split(x):
    hi = x.astype(BF16)
    return hi, (x - hi.astype(F32)).astype(BF16)


def dot3(a, b):
    ah, al = split(a)
    bh, bl = split(b)
    return dot16(
        jnp.concatenate([ah, ah, al], axis=1), jnp.concatenate([bh, bl, bh], axis=1), NT
    )


def sum_products(x, y):
    terms = [a * b for a, b in zip(x, y)]
    while len(terms) > 1:
        paired = [terms[i] + terms[i + 1] for i in range(0, len(terms) - 1, 2)]
        terms = paired + ([terms[-1]] if len(terms) % 2 else [])
    return terms[0]


class Block:
    def __init__(self, p):
        self.n = len(p)
        if self.n == 2:
            a, b, c = p[0][0], p[1][0], p[1][1]
            det = a * c - b * b
            q = 1.0 / det
            self.entries = (a, b, det)
            self.inverse = (c * q, -b * q, a * q)
            return
        h = self.n // 2
        self.first = Block([row[:h] for row in p[:h]])
        below = [[p[h + x][y] for y in range(h)] for x in range(h)]
        self.gain = [self.first.solve(row) for row in below]
        self.second = Block(
            [
                [p[h + x][h + y] - sum_products(self.gain[x], below[y]) for y in range(x + 1)]
                for x in range(h)
            ]
        )

    def reduce(self, rows):
        h = self.n // 2
        return [rows[h + x] - sum_products(self.gain[x], rows[:h]) for x in range(h)]

    def solve(self, rows):
        if self.n == 2:
            i00, i01, i11 = self.inverse
            return [i00 * rows[0] + i01 * rows[1], i01 * rows[0] + i11 * rows[1]]
        h = self.n // 2
        top = self.first.solve(rows[:h])
        bottom = self.second.solve(self.reduce(rows))
        top = [
            top[y] - sum_products([self.gain[x][y] for x in range(h)], bottom) for y in range(h)
        ]
        return top + bottom

    def half_solve(self, rows):
        if self.n == 2:
            a, b, det = self.entries
            scale = lax.rsqrt(a)
            inv_a = scale * scale
            return [
                rows[0] * scale,
                (rows[1] - (b * inv_a) * rows[0]) * lax.rsqrt(det * inv_a),
            ]
        return self.first.half_solve(rows[: self.n // 2]) + self.second.half_solve(
            self.reduce(rows)
        )


def factor_diagonal(tiles):
    tiles = list(tiles)
    lanes = lax.broadcasted_iota(jnp.int32, (8, 128), 1)
    subs = lax.broadcasted_iota(jnp.int32, (8, 128), 0)
    upper, inverse = [], []
    for v in range(16):
        j = 8 * v
        inside = (lanes >= j) & (lanes < j + SUBS)
        cols = [
            {i: jnp.broadcast_to(tiles[i][:, j + k : j + k + 1], (8, 128)) for i in range(v, 16)}
            for k in range(SUBS)
        ]
        rows = [jnp.broadcast_to(tiles[v][k : k + 1, :], (8, 128)) for k in range(SUBS)]
        pivots = [
            [jnp.broadcast_to(cols[l][v][k : k + 1, :], (8, 128)) for l in range(k + 1)]
            for k in range(SUBS)
        ]
        unit_rows = [
            jnp.where(inside, jnp.where(lanes == j + k, F32(1), F32(0)), rows[k])
            for k in range(SUBS)
        ]
        block = Block(pivots)
        solved = block.solve(unit_rows)
        up, inv = block.half_solve(rows), block.half_solve(unit_rows)
        up_tile, inv_tile = up[0], inv[0]
        for k in range(1, SUBS):
            up_tile = jnp.where(subs == k, up[k], up_tile)
            inv_tile = jnp.where(subs == k, inv[k], inv_tile)
        upper.append(jnp.where(lanes >= subs + j, up_tile, F32(0)))
        inverse.append(jnp.where(lanes <= subs + j, inv_tile, F32(0)))
        for i in range(v + 1, 16):
            tiles[i] = jnp.where(inside, F32(0), tiles[i]) - sum_products(
                [cols[k][i] for k in range(SUBS)], solved
            )
    return upper, inverse


AXES = ("x", "y", "z")
CUTS = ((0, 384), (384, 256), (640, 384))
ORDERS = (("y", "z", "x"), ("z", "x", "y"), ("x", "y", "z"))
LINKS = 144


class Mover:
    def __init__(self, send_sems, recv_sems):
        self.send_sems, self.recv_sems = send_sems, recv_sems
        row, col, grp = lax.axis_index("row"), lax.axis_index("col"), lax.axis_index("grp")
        self.row = row
        self.core = lax.rem(row, 2)
        self.at = {"x": row // 2, "y": grp * 2 + col // 4, "z": lax.rem(col, 4)}
        self.count = 0
        self.sent = []

    def device(self, axis, place):
        if axis == "x":
            return {"row": place * 2 + self.core}
        if axis == "y":
            return {"grp": place // 2, "col": lax.rem(place, 2) * 4 + self.at["z"]}
        return {"col": (self.at["y"] - self.at["y"] // 2 * 2) * 4 + place}

    def sibling(self):
        return {"row": self.row + 1 - 2 * self.core}

    def shifted(self, axis, by):
        return lax.rem(self.at[axis] + (by + 4), 4)

    def greet(self):
        barrier = pltpu.get_barrier_semaphore()
        others = [self.sibling()]
        for axis in AXES:
            others += [self.device(axis, self.shifted(axis, by)) for by in (1, 2, 3)]
        for other in others:
            pl.semaphore_signal(
                barrier, inc=1, device_id=other, device_id_type=pl.DeviceIdType.MESH
            )
        pl.semaphore_wait(barrier, len(others))

    def make(self, src, dst, device, send=True):
        i = self.count
        self.count += 1
        copy = pltpu.make_async_remote_copy(
            src_ref=src,
            dst_ref=dst,
            send_sem=self.send_sems.at[i],
            recv_sem=self.recv_sems.at[i],
            device_id=device,
            device_id_type=pl.DeviceIdType.MESH,
        )
        return copy

    def ring(self, axis, region, when=None):
        here = self.at[axis]
        ahead, behind = self.shifted(axis, 1), self.shifted(axis, -1)
        toward = lax.rem(here + 1 + 2 * self.core, 4)
        away = lax.rem(here + 3 - 2 * self.core, 4)
        plus = self.make(region(here), region(here), self.device(axis, ahead))
        minus = self.make(region(here), region(here), self.device(axis, behind))
        passed = self.make(region(away), region(away), self.device(axis, toward))
        self.sent += [(c, when) for c in (plus, minus, passed)]

        def first():
            plus.start()
            minus.start()

        def second():
            plus.wait_recv()
            minus.wait_recv()
            passed.start()

        def third():
            passed.wait_recv()

        return [guard(when, f) for f in (first, second, third)]

    def scatter(self, axis, source, target, when=None):
        here = self.at[axis]
        root, leaf = here == 0, here != 0
        if when is not None:
            root, leaf = root & when, leaf & when
        i = self.count
        self.count += 3
        recv = self.recv_sems.at[i]
        copies = []
        for k in (1, 2, 3):
            copies.append(
                pltpu.make_async_remote_copy(
                    src_ref=source(k),
                    dst_ref=target(k),
                    send_sem=self.send_sems.at[i + k - 1],
                    recv_sem=recv,
                    device_id=self.device(axis, k),
                    device_id_type=pl.DeviceIdType.MESH,
                )
            )
        self.sent += [(c, root) for c in copies]

        def first():
            for c in copies:
                c.start()

        def second():
            copies[0].wait_recv()

        return [guard(root, first), guard(leaf, second)]

    def push(self, region, when=None, taken=None):
        copy = self.make(region, region, self.sibling())
        self.sent.append((copy, when))
        return guard(when, copy.start), guard(taken, copy.wait_recv)

    def finish(self):
        for copy, when in self.sent:
            guard(when, copy.wait_send)()


def guard(when, f):
    if when is None:
        return f

    def guarded():
        pl.when(when)(f)

    return guarded


def merge(*steps):
    def run():
        for s in steps:
            s()

    return run


def rows_of(ref, start, count, cols=None):
    start = pl.multiple_of(start, 16)
    if cols is None:
        return ref.at[pl.ds(start, count)]
    return ref.at[pl.ds(start, count), pl.ds(*cols)]


def gather_program(
    raw, parent, g_ref, d_ref, st_ref, m_ref, u_ref, e_ref, lead, m_far, piece, e_y, e_z, st_a, sems
):
    send_sems, recv_sems, local_sems = sems
    mv = Mover(send_sems, recv_sems)
    x, y, z, core = mv.at["x"], mv.at["y"], mv.at["z"], mv.core
    locals_made = []

    def local(src, dst, when=None):
        copy = pltpu.make_async_copy(src, dst, local_sems.at[len(locals_made)])
        locals_made.append(copy)
        return guard(when, copy.start), guard(when, copy.wait)

    def block(place, cut):
        gy = (place["y"] // 2, lax.rem(place["y"], 2)) if "y" in place else (slice(None),) * 2
        px = place.get("x", slice(None))
        pz = place.get("z", slice(None))
        return g_ref.at[gy[0], px, core, gy[1], pz, :, pl.ds(*cut)]

    own = local(raw, g_ref.at[y // 2, x, core, lax.rem(y, 2), z])
    a_lists = []
    for cut, order in zip(CUTS, ORDERS):
        place = dict(mv.at)
        steps = []
        for stage, axis in enumerate(order):
            ring = mv.ring(axis, lambda k, p=dict(place), a=axis: block({**p, a: k}, cut))
            if stage == 2:
                base = mv.push(block(place, cut))
                near = [mv.push(block({**place, axis: mv.shifted(axis, by)}, cut)) for by in (1, 3)]
                far = mv.push(block({**place, axis: mv.shifted(axis, 2)}, cut))
                ring[0] = merge(ring[0], base[0])
                ring[1] = merge(ring[1], near[0][0], near[1][0])
                ring[2] = merge(ring[2], far[0])
                ring.append(merge(base[1], near[0][1], near[1][1], far[1]))
            steps += ring
            del place[axis]
        a_lists.append(steps)

    lead_core = core == 0
    part_d = lambda k: rows_of(d_ref, k * 256, 256)
    d_root = local(parent.at[pl.ds(0, 256)], d_ref.at[pl.ds(0, 256)], lead_core & (x == 0))
    hand = mv.scatter("x", lambda k: rows_of(parent, k * 256, 256), part_d, lead_core)
    turn = mv.ring("x", part_d, lead_core)
    push = mv.push(d_ref, lead_core, core == 1)
    d_steps = [
        merge(d_root[0], hand[0]),
        merge(d_root[1], hand[1], turn[0]),
        turn[1],
        merge(turn[2], push[0]),
        push[1],
    ]

    e_row = y * 256 + z * 64 + x * 16
    cut_x = lambda k: rows_of(e_ref, y * 256 + z * 64 + k * 16, 16)
    cut_z = lambda k: rows_of(e_ref, y * 256 + k * 64, 64)
    cut_y = lambda k: rows_of(e_ref, k * 256, 256)
    on_y = lead_core & (x == 0) & (z == 0)
    on_z = lead_core & (x == 0)
    loc_y = local(parent.at[pl.ds(0, 256)], e_y, on_y & (y == 0))
    loc_z = local(e_y.at[pl.ds(0, 64)], e_z, on_z & (z == 0))
    loc_x = local(e_z.at[pl.ds(0, 16)], rows_of(e_ref, e_row, 16), on_z)
    hand_y = mv.scatter("y", lambda k: rows_of(parent, k * 256, 256), lambda k: e_y, on_y)
    hand_z = mv.scatter("z", lambda k: e_y.at[pl.ds(64 * k, 64)], lambda k: e_z, on_z)
    hand_x = mv.scatter("x", lambda k: e_z.at[pl.ds(16 * k, 16)], cut_x, lead_core)
    turn_x = mv.ring("x", cut_x, lead_core)
    turn_z = mv.ring("z", cut_z, lead_core)
    turn_y = mv.ring("y", cut_y, lead_core)
    push = mv.push(e_ref, lead_core, core == 1)
    e_steps = [
        merge(loc_y[0], hand_y[0]),
        merge(loc_y[1], hand_y[1], loc_z[0], hand_z[0]),
        merge(loc_z[1], hand_z[1], loc_x[0], hand_x[0]),
        merge(loc_x[1], hand_x[1], turn_x[0]),
        turn_x[1],
        merge(turn_x[2], turn_z[0]),
        turn_z[1],
        merge(turn_z[2], turn_y[0]),
        turn_y[1],
        merge(turn_y[2], push[0]),
        push[1],
    ]

    st_lists = []
    for i, ((a, b), cut) in enumerate(((("z", "y"), (0, 512)), (("y", "z"), (512, 512)))):
        wide = lambda k, cut=cut: rows_of(st_ref, k * 512, 512, cut)
        wide_source = lambda k, cut=cut: rows_of(parent, k * 512, 512, cut)
        fine = lambda k, a=a, cut=cut: rows_of(st_ref, mv.at[a] * 512 + k * 128, 128, cut)
        held = st_a.at[i]
        line = mv.at[b] == 0
        loc_a = local(wide_source(0), held, line & (mv.at[a] == 0))
        loc_b = local(held.at[pl.ds(0, 128)], fine(0), line)
        hand_a = mv.scatter(a, wide_source, lambda k: held, line)
        hand_b = mv.scatter(b, lambda k: held.at[pl.ds(k * 128, 128)], fine)
        turn_b = mv.ring(b, fine)
        turn_a = mv.ring(a, wide)
        st_lists.append(
            [
                merge(loc_a[0], hand_a[0]),
                merge(loc_a[1], hand_a[1], loc_b[0], hand_b[0]),
                merge(loc_b[1], hand_b[1], turn_b[0]),
                turn_b[1],
                merge(turn_b[2], turn_a[0]),
                turn_a[1],
                turn_a[2],
            ]
        )

    y_lo = lax.rem(y, 2)
    base = core * (2 * 4 * raw.shape[0])
    size = raw.shape[0]
    chunk_z = lambda k: rows_of(u_ref, base + (y_lo * 4 + k) * size, size)
    u_own = local(raw, chunk_z(z), x == 0)
    u_hand = mv.scatter("x", lambda k: raw, lambda k: chunk_z(z))
    u_turn = mv.ring("z", chunk_z)
    full = 8 * size
    rest = e_ref.shape[0] - full
    beside = {"col": (1 - y_lo) * 4 + z}
    half = rows_of(u_ref, y_lo * 4 * size, 4 * size)
    swap = mv.make(half, half, beside)
    mv.sent.append((swap, lead_core))
    tail = u_ref.at[pl.ds(full, rest)]
    slide = mv.make(tail, tail, beside)
    mv.sent.append((slide, (core == 1) & (y_lo == 0)))
    push_head = mv.push(u_ref.at[pl.ds(0, full)], lead_core, core == 1)
    push_tail = mv.push(tail, core == 1, lead_core)
    u_steps = [
        merge(u_own[0], u_hand[0]),
        merge(u_own[1], u_hand[1], u_turn[0]),
        u_turn[1],
        merge(
            u_turn[2],
            guard(lead_core, swap.start),
            guard((core == 1) & (y_lo == 0), slide.start),
        ),
        merge(
            guard(lead_core, swap.wait_recv),
            guard((core == 1) & (y_lo == 1), slide.wait_recv),
            push_head[0],
            push_tail[0],
        ),
        merge(push_head[1], push_tail[1]),
    ]

    def exchange(mine, theirs):
        start = core * 512 + x * 128 + z * 32
        across = mv.make(mine(start, 32), theirs(start, 32), mv.device("y", mv.shifted("y", 2)))
        mv.sent.append((across, None))
        turn_z = mv.ring("z", lambda k: theirs(core * 512 + x * 128 + k * 32, 32))
        turn_x = mv.ring("x", lambda k: theirs(core * 512 + k * 128, 128))
        push = [
            mv.push(theirs(core * 512 + mv.shifted("x", by) * 128, 128)) for by in (0, 1, 3, 2)
        ]
        return [
            across.start,
            merge(across.wait_recv, turn_z[0]),
            turn_z[1],
            merge(turn_z[2], turn_x[0], push[0][0]),
            merge(turn_x[1], push[1][0], push[2][0]),
            merge(turn_x[2], push[3][0]),
            merge(*[p[1] for p in push]),
        ]

    def part(ref, *lead_index):
        return lambda start, n: ref.at[lead_index + (pl.ds(pl.multiple_of(start, 16), n),)]

    x_steps = exchange(lambda start, n: piece, part(lead, 1))
    m_steps = exchange(part(m_ref, slice(None)), part(m_far, slice(None)))
    assert mv.count <= LINKS
    a, st = [[merge(*s) for s in zip(*lists)] for lists in (a_lists, st_lists)]
    d, e, u, m = d_steps, e_steps, u_steps, m_steps
    early = [
        merge(mv.greet, own[0], u[0], e[0], own[1]),
        a[0],
        None,
        None,
        merge(u[1], e[1]),
        a[1],
        merge(u[2], e[2], a[2], a[3]),
        e[3],
        merge(u[3], e[4]),
        e[5],
        e[6],
        merge(e[7], a[4]),
        u[4],
        merge(a[5], d[0]),
        e[8],
        merge(e[9], u[5]),
    ]
    late = [
        merge(a[6], st[0]),
        d[1],
        m[0],
        None,
        None,
        m[1],
        merge(m[2], d[2]),
        st[1],
        m[3],
        a[7],
        merge(st[2], d[3]),
        m[4],
        st[3],
        m[5],
        a[8],
        st[4],
    ]
    last = [d[4], m[6], st[5], a[9], st[6]]
    return mv, early, x_steps, e[10], late, last


def factor_loop(w, inv_s, up_s, left, right, l_ref, ticks):
    width = w.shape[0]
    steps = width // NB
    if l_ref is not None:
        l_ref[...] = jnp.zeros_like(l_ref)

    def step(k, _):
        o = pl.multiple_of(k * NB, NB)
        here = pl.ds(o, NB)
        for i in range(0, len(ticks), 2):
            if ticks[i] is not None:
                pl.when(k == i // 2)(ticks[i])
        groups = [w[pl.ds(pl.multiple_of(o + 8 * i, 8), 8), here] for i in range(NB // 8)]
        up, inv = factor_diagonal(groups)
        for i in range(NB // 8):
            inv_s[8 * i : 8 * i + 8, :] = inv[i]
            up_s[8 * i : 8 * i + 8, :] = up[i]
        inverse = inv_s[...]
        panel = dot3(w[:, here], inverse)

        def clear(j, _):
            w[here, pl.ds(pl.multiple_of(j * NB, NB), NB)] = jnp.zeros((NB, NB), F32)
            return 0

        lax.fori_loop(k + 1, steps, clear, 0)
        w[:, here] = panel
        w[here, here] = inverse.T
        hi, lo = split(w[:, here])
        left[:, :NB] = hi
        left[:, NB : 2 * NB] = hi
        left[:, 2 * NB :] = lo
        right[:, :NB] = hi
        right[:, NB : 2 * NB] = lo
        right[:, 2 * NB :] = hi
        right[here, :] = jnp.zeros((NB, 3 * NB), BF16)
        if l_ref is not None:
            l_ref[here, here] = up_s[...].T

            def keep(j, _):
                below = pl.ds(pl.multiple_of(j * NB, NB), NB)
                l_ref[below, here] = w[below, here]
                return 0

            lax.fori_loop(k + 1, steps, keep, 0)
        for i in range(1, len(ticks), 2):
            if ticks[i] is not None:
                pl.when(k == i // 2)(ticks[i])

        def update(j, _):
            there = pl.ds(pl.multiple_of(j * CUT, CUT), CUT)
            w[:, there] -= dot16(left[...], right[there, :], NT)
            return 0

        lax.fori_loop((k + 1) * NB // CUT, width // CUT, update, 0)
        return 0

    lax.fori_loop(0, steps, step, 0)


def split_upper(w, m_ref):
    width = w.shape[0]
    for n in range(width // NB):
        cut = slice(n * NB, (n + 1) * NB)
        end = (n + 1) * NB
        hi, lo = split(w[:end, cut])
        m_ref[0, :end, cut] = hi
        m_ref[1, :end, cut] = lo
        if end < width:
            m_ref[:, end:, cut] = jnp.zeros((2, width - end, NB), BF16)


def apply_upper(rows, m_ref, cut):
    return dot16(rows, m_ref[0, : cut.stop, cut]) + dot16(rows, m_ref[1, : cut.stop, cut])


def front_kernel(
    a_ref, keep_ref, raw, parent,
    m_ref, m_pivot, l_ref, g_ref, d_ref, st_ref, lead_out, far_out,
    w, inv_s, up_s, left, right, u_ref, e_ref, lead, m_far, piece, e_y, e_z, st_a,
    send_sems, recv_sems, local_sems,
):
    width = a_ref.shape[0]
    mv, early, swap, pivot_here, late, last = gather_program(
        raw, parent, g_ref, d_ref, st_ref, m_ref, u_ref, e_ref, lead, m_far, piece, e_y, e_z,
        st_a, (send_sems, recv_sems, local_sems),
    )
    cuts = [slice(n, n + CUT) for n in range(0, width, CUT)]
    w[...] = a_ref[...]
    factor_loop(w, inv_s, up_s, left, right, None, early)
    split_upper(w, m_ref)
    mine = pl.ds(pl.multiple_of(mv.core * 512 + mv.at["x"] * 128 + mv.at["z"] * 32, 32), 32)
    for cut in cuts:
        both = apply_upper(u_ref[mine, : cut.stop], m_ref, cut)
        piece[:, cut] = (both * keep_ref[mine, :1]).astype(BF16)
    swap[0]()
    for cut in cuts:
        both = apply_upper(u_ref[:width, : cut.stop], m_ref, cut)
        lead[0, :, cut] = (both * keep_ref[:, :1]).astype(BF16)
    swap[1]()
    pivot_here()

    def subtract(i, cut, total):
        w[cut.start :, cut] = total - dot16(lead[i, cut.start :, :], lead[i, cut, :], NT)

    for n, cut in enumerate(cuts):
        if n == 1:
            swap[2]()
        if n == 3:
            swap[3]()
        subtract(0, cut, e_ref[cut.start :, cut].astype(F32))
    for step in swap[4:]:
        step()
    lead_copy = pltpu.make_async_copy(lead, lead_out, local_sems.at[14])
    far_copy = pltpu.make_async_copy(m_far, far_out, local_sems.at[15])
    lead_copy.start()
    for cut in cuts:
        subtract(1, cut, w[cut.start :, cut])
    factor_loop(w, inv_s, up_s, left, right, l_ref, late)
    split_upper(w, m_pivot)
    for step in last[:3]:
        step()
    far_copy.start()
    for step in last[3:]:
        step()
    mv.finish()
    lead_copy.wait()
    far_copy.wait()


def front(block, keep, raw, parent):
    width = block.shape[0]
    chunk = raw.shape[0]
    hbm = pl.BlockSpec(memory_space=pl.ANY)
    vmem = pl.BlockSpec(memory_space=VM)
    pair = jax.ShapeDtypeStruct((2, width, width), BF16)
    return pl.pallas_call(
        front_kernel,
        out_shape=[
            pair,
            pair,
            jax.ShapeDtypeStruct((width, width), F32),
            jax.ShapeDtypeStruct((2, 4, 2, 2, 4, chunk, width), BF16),
            jax.ShapeDtypeStruct((width, width), BF16),
            jax.ShapeDtypeStruct(parent.shape, BF16),
            pair,
            pair,
        ],
        in_specs=[vmem, vmem, hbm, hbm],
        out_specs=[vmem, vmem, vmem, hbm, hbm, hbm, hbm, hbm],
        scratch_shapes=[
            VM((width, width), F32),
            VM((NB, NB), F32),
            VM((NB, NB), F32),
            VM((width, 3 * NB), BF16),
            VM((width, 3 * NB), BF16),
            VM((16 * chunk, width), BF16),
            VM((width, width), BF16),
            VM((2, width, width), BF16),
            VM((2, width, width), BF16),
            VM((32, width), BF16),
            VM((256, width), BF16),
            VM((64, width), BF16),
            VM((2, 512, 512), BF16),
            pltpu.SemaphoreType.DMA((LINKS,)),
            pltpu.SemaphoreType.DMA((LINKS,)),
            pltpu.SemaphoreType.DMA((16,)),
        ],
        compiler_params=pltpu.CompilerParams(
            vmem_limit_bytes=52 * 2**20, collective_id=0, has_side_effects=True
        ),
        cost_estimate=pl.CostEstimate(
            flops=120_000_000_000, bytes_accessed=16 * width * width, transcendentals=0
        ),
        name="front",
    )(block, keep, raw, parent)


def chunk_span(chunk):
    return -(-(TB + chunk - 16) // chunk)


def finish_kernel(
    chunk, across, tile_ref, have_ref, flag_ref, gathered, own_hbm, far_hbm, lead_hbm, pivot_hbm,
    l_ref, d_ref, st_ref, parent_ref, out_ref,
    buf, sem, own, far, lead, pivot, load_sem, s_tile, b_tile, s_keep, f_keep,
):
    t = pl.program_id(0)
    tiles = pl.num_programs(0)
    width = b_tile.shape[1]
    span = chunk_span(chunk)
    slot = lax.rem(t, 2)

    def copies(t, slot):
        out = []
        for g in range(2):
            first = tile_ref[g * tiles + t] * TB // chunk
            for i in range(span):
                c = jnp.minimum(first + i, gathered.shape[1] - 1)
                out.append(
                    pltpu.make_async_copy(
                        gathered.at[g ^ flag_ref[2], c],
                        buf.at[slot, g, pl.ds(i * chunk, chunk)],
                        sem.at[slot, g, i],
                    )
                )
        return out

    loads = [
        pltpu.make_async_copy(src, dst, load_sem.at[i])
        for i, (src, dst) in enumerate(
            ((own_hbm, own), (lead_hbm, lead), (far_hbm, far), (pivot_hbm, pivot))
        )
    ]

    @pl.when(t == 0)
    def _():
        for c in copies(t, slot):
            c.start()
        for c in loads:
            c.start()

    @pl.when(t + 1 < tiles)
    def _():
        for c in copies(t + 1, 1 - slot):
            c.start()

    for c in copies(t, slot):
        c.wait()

    @pl.when(t < across)
    def _():
        b_tile[...] = d_ref[...].astype(F32).T

    @pl.when(t >= across)
    def _():
        b_tile[...] = st_ref[...].astype(F32)

    for g, m_ref in enumerate((own, far)):
        have = have_ref[g * tiles + t] != 0
        side = slice(g * width, (g + 1) * width)

        @pl.when(t == 0)
        def _():
            loads[2 * g].wait()
            if g == 0:
                loads[1].wait()

        @pl.when(jnp.logical_not(have))
        def _():
            s_tile[:, side] = jnp.zeros((TB, width), BF16)

        @pl.when(have)
        def _():
            off = pl.multiple_of(lax.rem(tile_ref[g * tiles + t] * TB, chunk), 16)
            for n in range(0, width, WIDE):
                cut = slice(n, n + WIDE)
                rows = buf[slot, g, pl.ds(off, TB), : n + WIDE]
                s_tile[:, g * width + n : g * width + n + WIDE] = apply_upper(
                    rows, m_ref, cut
                ).astype(BF16)
            b_tile[...] -= dot16(s_tile[:, side], lead[g], NT)

    @pl.when(t == 0)
    def _():
        loads[3].wait()

    b_hi, b_lo = split(b_tile[...])

    def panel(n):
        end = n + WIDE
        hi, lo = pivot[0, :end, n:end], pivot[1, :end, n:end]
        return dot16(b_hi[:, :end], hi) + dot16(b_hi[:, :end], lo) + dot16(b_lo[:, :end], hi)

    first = flag_ref[0] != 0
    lead_tile = (flag_ref[1] != 0) & (t < across + width // TB)
    below = t >= across

    @pl.when(jnp.logical_not(below))
    def _():
        here = pl.ds(pl.multiple_of(t * TB, TB), TB)
        s_keep[here, :] = s_tile[...]
        for n in range(0, width, WIDE):
            f_keep[here, n : n + WIDE] = panel(n).astype(BF16)

    @pl.when(below & first & lead_tile)
    def _():
        out_ref[...] = l_ref[...]

    @pl.when(below & first & jnp.logical_not(lead_tile))
    def _():
        for n in range(0, width, WIDE):
            out_ref[:, n : n + WIDE] = panel(n)

    @pl.when(below & jnp.logical_not(first) & lead_tile)
    def _():
        out_ref[...] = jnp.zeros_like(out_ref)

    @pl.when(below & jnp.logical_not(first) & jnp.logical_not(lead_tile))
    def _():
        f = jnp.concatenate([panel(n).astype(BF16) for n in range(0, width, WIDE)], axis=1)
        out_ref[...] = parent_ref[...].astype(F32) - (
            dot16(s_tile[...], s_keep[...], NT) + dot16(f, f_keep[...], NT)
        )


def finish(tiles, have, flags, gathered, m_own, m_far, lead_both, m_pivot, factor, panel, stripe, parent):
    chunk = gathered.shape[2]
    width = lead_both.shape[-1]
    cols = parent.shape[1]
    across = cols // TB
    lead = width // TB
    grid = across + parent.shape[0] // TB
    hbm = pl.BlockSpec(memory_space=pl.ANY)
    pair = VM((2, width, width), BF16)
    stripe_at = lambda t, *_: (jnp.maximum(t - across, 0), 0)
    return pl.pallas_call(
        functools.partial(finish_kernel, chunk, across),
        grid_spec=pltpu.PrefetchScalarGridSpec(
            num_scalar_prefetch=3,
            grid=(grid,),
            in_specs=[
                hbm,
                hbm,
                hbm,
                hbm,
                hbm,
                pl.BlockSpec((TB, width), lambda t, *_: (jnp.clip(t - across, 0, lead - 1), 0)),
                pl.BlockSpec((width, TB), lambda t, *_: (0, jnp.minimum(t, across - 1))),
                pl.BlockSpec((TB, width), stripe_at),
                pl.BlockSpec((TB, cols), stripe_at),
            ],
            out_specs=pl.BlockSpec((TB, cols), stripe_at),
            scratch_shapes=[
                VM((2, 2, chunk_span(chunk) * chunk, width), BF16),
                pltpu.SemaphoreType.DMA((2, 2, chunk_span(chunk))),
                pair,
                pair,
                pair,
                pair,
                pltpu.SemaphoreType.DMA((4,)),
                VM((TB, 2 * width), BF16),
                VM((TB, width), F32),
                VM((cols, 2 * width), BF16),
                VM((cols, width), BF16),
            ],
        ),
        out_shape=jax.ShapeDtypeStruct(parent.shape, F32),
        compiler_params=pltpu.CompilerParams(vmem_limit_bytes=56 * 2**20),
        cost_estimate=pl.CostEstimate(
            flops=60_000_000_000, bytes_accessed=60 * 2**20, transcendentals=0
        ),
        name="finish",
    )(tiles, have, flags, gathered, m_own, m_far, lead_both, m_pivot, factor, panel, stripe, parent)


def locate(tile_map, parent_tiles):
    matches = tile_map[:, None] == jnp.arange(parent_tiles, dtype=jnp.int32)[None, :]
    positions = jnp.arange(tile_map.shape[0], dtype=jnp.int32)[:, None]
    return jnp.sum(jnp.where(matches, positions, 0), axis=0), jnp.any(matches, axis=0)


def per_device(child_update, child_pivot, child_map, parent_front):
    width = child_pivot.shape[-1]
    stripe_rows, block_cols = parent_front.shape
    row_tiles = stripe_rows // TB
    col_tiles = block_cols // TB
    parent_tiles = row_tiles * lax.axis_size("row")
    row = lax.axis_index("row")
    block = lax.axis_index(("grp", "col"))
    raw = child_update[0]
    chunk = raw.shape[0]

    grp = lax.axis_index("grp")
    own_map = jnp.where(grp == 0, child_map, child_map[::-1])
    lead_tiles = jnp.arange(width // TB, dtype=jnp.int32)
    keep = (own_map[0, : width // TB] == lead_tiles).astype(F32)
    keep = jnp.broadcast_to(jnp.repeat(keep, TB)[:, None], (width, 128))
    m_own, m_pivot, pivot_factor, gathered, column_panel, stripe, lead_both, m_far = front(
        child_pivot[0], keep, raw, parent_front
    )
    gathered = gathered.reshape(2, -1, chunk, width)

    wanted_tiles = jnp.concatenate(
        [
            block * col_tiles + jnp.arange(col_tiles, dtype=jnp.int32),
            row * row_tiles + jnp.arange(row_tiles, dtype=jnp.int32),
        ]
    )
    tiles, have = [], []
    for g in range(2):
        inverse, present = locate(own_map[g], parent_tiles)
        tiles.append(inverse[wanted_tiles])
        have.append(present[wanted_tiles].astype(jnp.int32))
    tiles, have = jnp.concatenate(tiles), jnp.concatenate(have)
    flags = jnp.stack([block == 0, row == 0, grp == 1]).astype(jnp.int32)
    return finish(
        tiles, have, flags, gathered, m_own, m_far, lead_both, m_pivot, pivot_factor,
        column_panel, stripe, parent_front,
    )


def solution(mesh):
    in_specs = (P("grp", ("row", "col"), None), P("grp", None, None), P(), P("row", ("grp", "col")))
    out_specs = P("row", ("grp", "col"))
    return jax.shard_map(
        per_device, mesh=mesh, in_specs=in_specs, out_specs=out_specs, check_vma=False
    )
```

```python
import functools

import jax
import jax.numpy as jnp
from jax import lax
from jax.experimental import pallas as pl
from jax.experimental.pallas import tpu as pltpu
from jax.sharding import PartitionSpec as P

TB = 512
F32 = jnp.float32
BF16 = jnp.bfloat16
NB = 128
SUBS = 8
VM = pltpu.VMEM
NT = (((1,), (1,)), ((), ()))
NN = (((1,), (0,)), ((), ()))


CUT = 256
WIDE = 512


def dot16(a, b, dims=NN):
    return lax.dot_general(a, b, dims, preferred_element_type=F32)


def split(x):
    hi = x.astype(BF16)
    return hi, (x - hi.astype(F32)).astype(BF16)


def dot3(a, b):
    ah, al = split(a)
    bh, bl = split(b)
    return dot16(
        jnp.concatenate([ah, ah, al], axis=1), jnp.concatenate([bh, bl, bh], axis=1), NT
    )


def sum_products(x, y):
    terms = [a * b for a, b in zip(x, y)]
    while len(terms) > 1:
        paired = [terms[i] + terms[i + 1] for i in range(0, len(terms) - 1, 2)]
        terms = paired + ([terms[-1]] if len(terms) % 2 else [])
    return terms[0]


class Block:
    def __init__(self, p):
        self.n = len(p)
        if self.n == 2:
            a, b, c = p[0][0], p[1][0], p[1][1]
            det = a * c - b * b
            q = 1.0 / det
            self.entries = (a, b, det)
            self.inverse = (c * q, -b * q, a * q)
            return
        h = self.n // 2
        self.first = Block([row[:h] for row in p[:h]])
        below = [[p[h + x][y] for y in range(h)] for x in range(h)]
        self.gain = [self.first.solve(row) for row in below]
        self.second = Block(
            [
                [p[h + x][h + y] - sum_products(self.gain[x], below[y]) for y in range(x + 1)]
                for x in range(h)
            ]
        )

    def reduce(self, rows):
        h = self.n // 2
        return [rows[h + x] - sum_products(self.gain[x], rows[:h]) for x in range(h)]

    def solve(self, rows):
        if self.n == 2:
            i00, i01, i11 = self.inverse
            return [i00 * rows[0] + i01 * rows[1], i01 * rows[0] + i11 * rows[1]]
        h = self.n // 2
        top = self.first.solve(rows[:h])
        bottom = self.second.solve(self.reduce(rows))
        top = [
            top[y] - sum_products([self.gain[x][y] for x in range(h)], bottom) for y in range(h)
        ]
        return top + bottom

    def half_solve(self, rows):
        if self.n == 2:
            a, b, det = self.entries
            scale = lax.rsqrt(a)
            inv_a = scale * scale
            return [
                rows[0] * scale,
                (rows[1] - (b * inv_a) * rows[0]) * lax.rsqrt(det * inv_a),
            ]
        return self.first.half_solve(rows[: self.n // 2]) + self.second.half_solve(
            self.reduce(rows)
        )


def factor_diagonal(tiles):
    tiles = list(tiles)
    lanes = lax.broadcasted_iota(jnp.int32, (8, 128), 1)
    subs = lax.broadcasted_iota(jnp.int32, (8, 128), 0)
    upper, inverse = [], []
    for v in range(16):
        j = 8 * v
        inside = (lanes >= j) & (lanes < j + SUBS)
        cols = [
            {i: jnp.broadcast_to(tiles[i][:, j + k : j + k + 1], (8, 128)) for i in range(v, 16)}
            for k in range(SUBS)
        ]
        rows = [jnp.broadcast_to(tiles[v][k : k + 1, :], (8, 128)) for k in range(SUBS)]
        pivots = [
            [jnp.broadcast_to(cols[l][v][k : k + 1, :], (8, 128)) for l in range(k + 1)]
            for k in range(SUBS)
        ]
        unit_rows = [
            jnp.where(inside, jnp.where(lanes == j + k, F32(1), F32(0)), rows[k])
            for k in range(SUBS)
        ]
        block = Block(pivots)
        solved = block.solve(unit_rows)
        up, inv = block.half_solve(rows), block.half_solve(unit_rows)
        up_tile, inv_tile = up[0], inv[0]
        for k in range(1, SUBS):
            up_tile = jnp.where(subs == k, up[k], up_tile)
            inv_tile = jnp.where(subs == k, inv[k], inv_tile)
        upper.append(jnp.where(lanes >= subs + j, up_tile, F32(0)))
        inverse.append(jnp.where(lanes <= subs + j, inv_tile, F32(0)))
        for i in range(v + 1, 16):
            tiles[i] = jnp.where(inside, F32(0), tiles[i]) - sum_products(
                [cols[k][i] for k in range(SUBS)], solved
            )
    return upper, inverse


AXES = ("x", "y", "z")
CUTS = ((0, 48), (48, 32), (80, 32))
ORDERS = (("y", "z", "x"), ("z", "x", "y"), ("x", "y", "z"))
LINKS = 144


class Mover:
    def __init__(self, send_sems, recv_sems):
        self.send_sems, self.recv_sems = send_sems, recv_sems
        row, col, grp = lax.axis_index("row"), lax.axis_index("col"), lax.axis_index("grp")
        self.row = row
        self.core = lax.rem(row, 2)
        self.at = {"x": row // 2, "y": grp * 2 + col // 4, "z": lax.rem(col, 4)}
        self.count = 0
        self.sent = []

    def device(self, axis, place):
        if axis == "x":
            return {"row": place * 2 + self.core}
        if axis == "y":
            return {"grp": place // 2, "col": lax.rem(place, 2) * 4 + self.at["z"]}
        return {"col": (self.at["y"] - self.at["y"] // 2 * 2) * 4 + place}

    def sibling(self):
        return {"row": self.row + 1 - 2 * self.core}

    def shifted(self, axis, by):
        return lax.rem(self.at[axis] + (by + 4), 4)

    def greet(self):
        barrier = pltpu.get_barrier_semaphore()
        others = [self.sibling()]
        for axis in AXES:
            others += [self.device(axis, self.shifted(axis, by)) for by in (1, 2, 3)]
        for other in others:
            pl.semaphore_signal(
                barrier, inc=1, device_id=other, device_id_type=pl.DeviceIdType.MESH
            )
        pl.semaphore_wait(barrier, len(others))

    def make(self, src, dst, device, send=True):
        i = self.count
        self.count += 1
        copy = pltpu.make_async_remote_copy(
            src_ref=src,
            dst_ref=dst,
            send_sem=self.send_sems.at[i],
            recv_sem=self.recv_sems.at[i],
            device_id=device,
            device_id_type=pl.DeviceIdType.MESH,
        )
        return copy

    def ring(self, axis, region, when=None):
        here = self.at[axis]
        ahead, behind = self.shifted(axis, 1), self.shifted(axis, -1)
        toward = lax.rem(here + 1 + 2 * self.core, 4)
        away = lax.rem(here + 3 - 2 * self.core, 4)
        plus = self.make(region(here), region(here), self.device(axis, ahead))
        minus = self.make(region(here), region(here), self.device(axis, behind))
        passed = self.make(region(away), region(away), self.device(axis, toward))
        self.sent += [(c, when) for c in (plus, minus, passed)]

        def first():
            plus.start()
            minus.start()

        def second():
            plus.wait_recv()
            minus.wait_recv()
            passed.start()

        def third():
            passed.wait_recv()

        return [guard(when, f) for f in (first, second, third)]

    def line(self, axis, region, when=None):
        here = self.at[axis]
        copies = [
            self.make(region(here), region(here), self.device(axis, self.shifted(axis, by)))
            for by in (1, 3, 2)
        ]
        self.sent += [(c, when) for c in copies]

        def first():
            for c in copies:
                c.start()

        def second():
            for c in copies:
                c.wait_recv()

        return [guard(when, first), guard(when, second)]

    def scatter(self, axis, source, target, when=None):
        here = self.at[axis]
        root, leaf = here == 0, here != 0
        if when is not None:
            root, leaf = root & when, leaf & when
        i = self.count
        self.count += 3
        recv = self.recv_sems.at[i]
        copies = []
        for k in (1, 2, 3):
            copies.append(
                pltpu.make_async_remote_copy(
                    src_ref=source(k),
                    dst_ref=target(k),
                    send_sem=self.send_sems.at[i + k - 1],
                    recv_sem=recv,
                    device_id=self.device(axis, k),
                    device_id_type=pl.DeviceIdType.MESH,
                )
            )
        self.sent += [(c, root) for c in copies]

        def first():
            for c in copies:
                c.start()

        def second():
            copies[0].wait_recv()

        return [guard(root, first), guard(leaf, second)]

    def push(self, region, when=None, taken=None):
        copy = self.make(region, region, self.sibling())
        self.sent.append((copy, when))
        return guard(when, copy.start), guard(taken, copy.wait_recv)

    def finish(self):
        for copy, when in self.sent:
            guard(when, copy.wait_send)()


def guard(when, f):
    if when is None:
        return f

    def guarded():
        pl.when(when)(f)

    return guarded


def merge(*steps):
    def run():
        for s in steps:
            s()

    return run


def rows_of(ref, start, count, cols=None):
    start = pl.multiple_of(start, 16)
    if cols is None:
        return ref.at[pl.ds(start, count)]
    return ref.at[pl.ds(start, count), pl.ds(*cols)]


def gather_program(
    raw, parent, g_ref, d_ref, st_ref, m_ref, u_ref, e_ref, lead, m_far, piece, e_y, e_z, st_a, sems
):
    send_sems, recv_sems, local_sems = sems
    mv = Mover(send_sems, recv_sems)
    x, y, z, core = mv.at["x"], mv.at["y"], mv.at["z"], mv.core
    locals_made = []

    def local(src, dst, when=None):
        copy = pltpu.make_async_copy(src, dst, local_sems.at[len(locals_made)])
        locals_made.append(copy)
        return guard(when, copy.start), guard(when, copy.wait)

    def block(place, cut):
        gy = (place["y"] // 2, lax.rem(place["y"], 2)) if "y" in place else (slice(None),) * 2
        px = place.get("x", slice(None))
        pz = place.get("z", slice(None))
        return g_ref.at[gy[0], px, core, gy[1], pz, pl.ds(*cut)]

    own = local(raw, g_ref.at[y // 2, x, core, lax.rem(y, 2), z])
    a_lists = []
    for cut, order in zip(CUTS, ORDERS):
        place = dict(mv.at)
        steps = []
        for stage, axis in enumerate(order):
            ring = mv.ring(axis, lambda k, p=dict(place), a=axis: block({**p, a: k}, cut))
            if stage == 2:
                base = mv.push(block(place, cut))
                near = [mv.push(block({**place, axis: mv.shifted(axis, by)}, cut)) for by in (1, 3)]
                far = mv.push(block({**place, axis: mv.shifted(axis, 2)}, cut))
                ring[0] = merge(ring[0], base[0])
                ring[1] = merge(ring[1], near[0][0], near[1][0])
                ring[2] = merge(ring[2], far[0])
                ring.append(merge(base[1], near[0][1], near[1][1], far[1]))
            steps += ring
            del place[axis]
        a_lists.append(steps)

    lead_core = core == 0
    part_d = lambda k: rows_of(d_ref, k * 256, 256)
    d_root = local(parent.at[pl.ds(0, 256)], d_ref.at[pl.ds(0, 256)], lead_core & (x == 0))
    hand = mv.scatter("x", lambda k: rows_of(parent, k * 256, 256), part_d, lead_core)
    turn = mv.ring("x", part_d, lead_core)
    push = mv.push(d_ref, lead_core, core == 1)
    d_steps = [
        merge(d_root[0], hand[0]),
        merge(d_root[1], hand[1], turn[0]),
        turn[1],
        merge(turn[2], push[0]),
        push[1],
    ]

    cut_z = lambda k: rows_of(e_ref, y * 256 + k * 64, 64)
    cut_y = lambda k: rows_of(e_ref, k * 256, 256)
    on_y = lead_core & (x == 0) & (z == 0)
    on_z = lead_core & (x == 0)
    loc_y = local(parent.at[pl.ds(0, 256)], e_y, on_y & (y == 0))
    loc_z = local(e_y.at[pl.ds(0, 64)], e_z, on_z & (z == 0))
    loc_x = local(e_z, cut_z(z), on_z)
    hand_y = mv.scatter("y", lambda k: rows_of(parent, k * 256, 256), lambda k: e_y, on_y)
    hand_z = mv.scatter("z", lambda k: e_y.at[pl.ds(64 * k, 64)], lambda k: e_z, on_z)
    hand_x = mv.scatter("x", lambda k: e_z, lambda k: cut_z(z), lead_core)
    turn_z = mv.line("z", cut_z, lead_core)
    turn_y = mv.line("y", cut_y, lead_core)
    push = mv.push(e_ref, lead_core, core == 1)
    e_steps = [
        merge(loc_y[0], hand_y[0]),
        merge(loc_y[1], hand_y[1], loc_z[0], hand_z[0]),
        merge(loc_z[1], hand_z[1], loc_x[0], hand_x[0]),
        merge(loc_x[1], hand_x[1], turn_z[0]),
        merge(turn_z[1], turn_y[0]),
        merge(turn_y[1], push[0]),
        push[1],
    ]

    st_lists = []
    for i, (a, b) in enumerate((("z", "y"), ("y", "z"))):
        wide = lambda k, i=i: rows_of(st_ref, k * 512 + i * 256, 256)
        wide_source = lambda k, i=i: rows_of(parent, k * 512 + i * 256, 256)
        fine = lambda k, a=a, i=i: rows_of(st_ref, mv.at[a] * 512 + i * 256 + k * 64, 64)
        held = st_a.at[i]
        line = mv.at[b] == 0
        loc_a = local(wide_source(0), held, line & (mv.at[a] == 0))
        loc_b = local(held.at[pl.ds(0, 64)], fine(0), line)
        hand_a = mv.scatter(a, wide_source, lambda k: held, line)
        hand_b = mv.scatter(b, lambda k: held.at[pl.ds(k * 64, 64)], fine)
        turn_b = mv.ring(b, fine)
        turn_a = mv.ring(a, wide)
        st_lists.append(
            [
                merge(loc_a[0], hand_a[0]),
                merge(loc_a[1], hand_a[1], loc_b[0], hand_b[0]),
                merge(loc_b[1], hand_b[1], turn_b[0]),
                turn_b[1],
                merge(turn_b[2], turn_a[0]),
                turn_a[1],
                turn_a[2],
            ]
        )

    y_lo = lax.rem(y, 2)
    base = core * (2 * 4 * raw.shape[0])
    size = raw.shape[0]
    chunk_z = lambda k: rows_of(u_ref, base + (y_lo * 4 + k) * size, size)
    u_own = local(raw, chunk_z(z), x == 0)
    u_hand = mv.scatter("x", lambda k: raw, lambda k: chunk_z(z))
    u_turn = mv.line("z", chunk_z)
    full = 8 * size
    rest = e_ref.shape[0] - full
    beside = {"col": (1 - y_lo) * 4 + z}
    half = rows_of(u_ref, y_lo * 4 * size, 4 * size)
    swap = mv.make(half, half, beside)
    mv.sent.append((swap, lead_core))
    tail = u_ref.at[pl.ds(full, rest)]
    slide = mv.make(tail, tail, beside)
    mv.sent.append((slide, (core == 1) & (y_lo == 0)))
    push_head = mv.push(u_ref.at[pl.ds(0, full)], lead_core, core == 1)
    push_tail = mv.push(tail, core == 1, lead_core)
    u_steps = [
        merge(u_own[0], u_hand[0]),
        merge(u_own[1], u_hand[1], u_turn[0]),
        merge(
            u_turn[1],
            guard(lead_core, swap.start),
            guard((core == 1) & (y_lo == 0), slide.start),
        ),
        merge(
            guard(lead_core, swap.wait_recv),
            guard((core == 1) & (y_lo == 1), slide.wait_recv),
            push_head[0],
            push_tail[0],
        ),
        merge(push_head[1], push_tail[1]),
    ]

    def exchange(mine, theirs, direct):
        start = core * 512 + x * 128 + z * 32
        across = mv.make(mine(start, 32), theirs(start, 32), mv.device("y", mv.shifted("y", 2)))
        mv.sent.append((across, None))
        turn = mv.line if direct else mv.ring
        turn_z = turn("z", lambda k: theirs(core * 512 + x * 128 + k * 32, 32))
        turn_x = turn("x", lambda k: theirs(core * 512 + k * 128, 128))
        push = [
            mv.push(theirs(core * 512 + mv.shifted("x", by) * 128, 128)) for by in (0, 1, 3, 2)
        ]
        if direct:
            return [
                across.start,
                merge(across.wait_recv, turn_z[0]),
                merge(turn_z[1], turn_x[0], push[0][0]),
                merge(turn_x[1], push[1][0], push[2][0], push[3][0]),
                merge(*[p[1] for p in push]),
            ]
        return [
            across.start,
            merge(across.wait_recv, turn_z[0]),
            turn_z[1],
            merge(turn_z[2], turn_x[0], push[0][0]),
            merge(turn_x[1], push[1][0], push[2][0]),
            merge(turn_x[2], push[3][0]),
            merge(*[p[1] for p in push]),
        ]

    def part(ref, *lead_index):
        return lambda start, n: ref.at[lead_index + (pl.ds(pl.multiple_of(start, 16), n),)]

    x_steps = exchange(lambda start, n: piece, part(lead, 1), True)
    m_steps = exchange(part(m_ref, slice(None)), part(m_far, slice(None)), False)
    assert mv.count <= LINKS
    a, st = [[merge(*s) for s in zip(*lists)] for lists in (a_lists, st_lists)]
    d, e, u, m = d_steps, e_steps, u_steps, m_steps
    early = [
        merge(mv.greet, own[0], u[0], e[0], own[1]),
        a[0],
        None,
        None,
        None,
        merge(u[1], e[1]),
        a[1],
        e[2],
        merge(a[2], a[3]),
        e[3],
        u[2],
        e[4],
        a[4],
        d[0],
        merge(u[3], a[5]),
        merge(e[5], u[4]),
    ]
    late = [
        merge(a[6], st[0]),
        d[1],
        m[0],
        None,
        None,
        m[1],
        merge(m[2], d[2]),
        st[1],
        m[3],
        a[7],
        merge(st[2], d[3]),
        m[4],
        st[3],
        m[5],
        a[8],
        st[4],
    ]
    last = [d[4], m[6], st[5], a[9], st[6]]
    return mv, early, x_steps, e[6], late, last


def factor_loop(w, inv_s, up_s, left, right, l_ref, ticks):
    width = w.shape[0]
    steps = width // NB
    if l_ref is not None:
        l_ref[...] = jnp.zeros_like(l_ref)

    def step(k, _):
        o = pl.multiple_of(k * NB, NB)
        here = pl.ds(o, NB)
        for i in range(0, len(ticks), 2):
            if ticks[i] is not None:
                pl.when(k == i // 2)(ticks[i])
        groups = [w[pl.ds(pl.multiple_of(o + 8 * i, 8), 8), here] for i in range(NB // 8)]
        up, inv = factor_diagonal(groups)
        for i in range(NB // 8):
            inv_s[8 * i : 8 * i + 8, :] = inv[i]
            up_s[8 * i : 8 * i + 8, :] = up[i]
        inverse = inv_s[...]
        panel = dot3(w[:, here], inverse)

        def clear(j, _):
            w[here, pl.ds(pl.multiple_of(j * NB, NB), NB)] = jnp.zeros((NB, NB), F32)
            return 0

        lax.fori_loop(k + 1, steps, clear, 0)
        w[:, here] = panel
        w[here, here] = inverse.T
        hi, lo = split(w[:, here])
        left[:, :NB] = hi
        left[:, NB : 2 * NB] = hi
        left[:, 2 * NB :] = lo
        right[:, :NB] = hi
        right[:, NB : 2 * NB] = lo
        right[:, 2 * NB :] = hi
        right[here, :] = jnp.zeros((NB, 3 * NB), BF16)
        if l_ref is not None:
            l_ref[here, here] = up_s[...].T

            def keep(j, _):
                below = pl.ds(pl.multiple_of(j * NB, NB), NB)
                l_ref[below, here] = w[below, here]
                return 0

            lax.fori_loop(k + 1, steps, keep, 0)
        for i in range(1, len(ticks), 2):
            if ticks[i] is not None:
                pl.when(k == i // 2)(ticks[i])

        def update(j, _):
            there = pl.ds(pl.multiple_of(j * CUT, CUT), CUT)
            w[:, there] -= dot16(left[...], right[there, :], NT)
            return 0

        lax.fori_loop((k + 1) * NB // CUT, width // CUT, update, 0)
        return 0

    lax.fori_loop(0, steps, step, 0)


def split_upper(w, m_ref):
    width = w.shape[0]
    for n in range(width // NB):
        cut = slice(n * NB, (n + 1) * NB)
        end = (n + 1) * NB
        hi, lo = split(w[:end, cut])
        m_ref[0, :end, cut] = hi
        m_ref[1, :end, cut] = lo
        if end < width:
            m_ref[:, end:, cut] = jnp.zeros((2, width - end, NB), BF16)


def apply_upper(rows, m_ref, cut):
    return dot16(rows, m_ref[0, : cut.stop, cut]) + dot16(rows, m_ref[1, : cut.stop, cut])


def front_kernel(
    a_ref, keep_ref, raw, parent,
    m_ref, m_pivot, l_ref, g_ref, d_ref, st_ref, lead_out, far_out,
    w, inv_s, up_s, left, right, u_ref, e_ref, lead, m_far, piece, e_y, e_z, st_a,
    send_sems, recv_sems, local_sems,
):
    width = a_ref.shape[0]
    mv, early, swap, pivot_here, late, last = gather_program(
        raw, parent, g_ref, d_ref, st_ref, m_ref, u_ref, e_ref, lead, m_far, piece, e_y, e_z,
        st_a, (send_sems, recv_sems, local_sems),
    )
    cuts = [slice(n, n + CUT) for n in range(0, width, CUT)]
    w[...] = a_ref[...]
    factor_loop(w, inv_s, up_s, left, right, None, early)
    split_upper(w, m_ref)
    mine = pl.ds(pl.multiple_of(mv.core * 512 + mv.at["x"] * 128 + mv.at["z"] * 32, 32), 32)
    for cut in cuts:
        both = apply_upper(u_ref[mine, : cut.stop], m_ref, cut)
        piece[:, cut] = (both * keep_ref[mine, :1]).astype(BF16)
    swap[0]()
    for cut in cuts:
        both = apply_upper(u_ref[:width, : cut.stop], m_ref, cut)
        lead[0, :, cut] = (both * keep_ref[:, :1]).astype(BF16)
    swap[1]()
    pivot_here()

    def subtract(i, cut, total):
        w[cut.start :, cut] = total - dot16(lead[i, cut.start :, :], lead[i, cut, :], NT)

    for n, cut in enumerate(cuts):
        if n == 1:
            swap[2]()
        subtract(0, cut, e_ref[cut.start :, cut].astype(F32))
    for step in swap[3:]:
        step()
    lead_copy = pltpu.make_async_copy(lead, lead_out, local_sems.at[14])
    far_copy = pltpu.make_async_copy(m_far, far_out, local_sems.at[15])
    lead_copy.start()
    for cut in cuts:
        subtract(1, cut, w[cut.start :, cut])
    factor_loop(w, inv_s, up_s, left, right, l_ref, late)
    split_upper(w, m_pivot)
    for step in last[:3]:
        step()
    far_copy.start()
    for step in last[3:]:
        step()
    mv.finish()
    lead_copy.wait()
    far_copy.wait()


def front(block, keep, raw, parent):
    width = block.shape[0]
    chunk = raw.shape[0]
    hbm = pl.BlockSpec(memory_space=pl.ANY)
    vmem = pl.BlockSpec(memory_space=VM)
    pair = jax.ShapeDtypeStruct((2, width, width), BF16)
    return pl.pallas_call(
        front_kernel,
        out_shape=[
            pair,
            pair,
            jax.ShapeDtypeStruct((width, width), F32),
            jax.ShapeDtypeStruct((2, 4, 2, 2, 4, chunk, width), BF16),
            jax.ShapeDtypeStruct((width, width), BF16),
            jax.ShapeDtypeStruct(parent.shape, BF16),
            pair,
            pair,
        ],
        in_specs=[vmem, vmem, hbm, hbm],
        out_specs=[vmem, vmem, vmem, hbm, hbm, hbm, hbm, hbm],
        scratch_shapes=[
            VM((width, width), F32),
            VM((NB, NB), F32),
            VM((NB, NB), F32),
            VM((width, 3 * NB), BF16),
            VM((width, 3 * NB), BF16),
            VM((16 * chunk, width), BF16),
            VM((width, width), BF16),
            VM((2, width, width), BF16),
            VM((2, width, width), BF16),
            VM((32, width), BF16),
            VM((256, width), BF16),
            VM((64, width), BF16),
            VM((2, 256, width), BF16),
            pltpu.SemaphoreType.DMA((LINKS,)),
            pltpu.SemaphoreType.DMA((LINKS,)),
            pltpu.SemaphoreType.DMA((16,)),
        ],
        compiler_params=pltpu.CompilerParams(
            vmem_limit_bytes=52 * 2**20, collective_id=0, has_side_effects=True
        ),
        cost_estimate=pl.CostEstimate(
            flops=120_000_000_000, bytes_accessed=16 * width * width, transcendentals=0
        ),
        name="front",
    )(block, keep, raw, parent)


def chunk_span(chunk):
    return -(-(TB + chunk - 16) // chunk)


def finish_kernel(
    chunk, across, tile_ref, have_ref, flag_ref, gathered, own_hbm, far_hbm, lead_hbm, pivot_hbm,
    l_ref, d_ref, st_ref, parent_ref, out_ref,
    buf, sem, own, far, lead, pivot, load_sem, s_tile, b_tile, s_keep, f_keep,
):
    t = pl.program_id(0)
    tiles = pl.num_programs(0)
    width = b_tile.shape[1]
    span = chunk_span(chunk)
    slot = lax.rem(t, 2)

    def copies(t, slot):
        out = []
        for g in range(2):
            first = tile_ref[g * tiles + t] * TB // chunk
            for i in range(span):
                c = jnp.minimum(first + i, gathered.shape[1] - 1)
                out.append(
                    pltpu.make_async_copy(
                        gathered.at[g ^ flag_ref[2], c],
                        buf.at[slot, g, pl.ds(i * chunk, chunk)],
                        sem.at[slot, g, i],
                    )
                )
        return out

    loads = [
        pltpu.make_async_copy(src, dst, load_sem.at[i])
        for i, (src, dst) in enumerate(
            ((own_hbm, own), (lead_hbm, lead), (far_hbm, far), (pivot_hbm, pivot))
        )
    ]

    @pl.when(t == 0)
    def _():
        for c in copies(t, slot):
            c.start()
        for c in loads:
            c.start()

    @pl.when(t + 1 < tiles)
    def _():
        for c in copies(t + 1, 1 - slot):
            c.start()

    for c in copies(t, slot):
        c.wait()

    @pl.when(t < across)
    def _():
        b_tile[...] = d_ref[...].astype(F32).T

    @pl.when(t >= across)
    def _():
        b_tile[...] = st_ref[...].astype(F32)

    for g, m_ref in enumerate((own, far)):
        have = have_ref[g * tiles + t] != 0
        side = slice(g * width, (g + 1) * width)

        @pl.when(t == 0)
        def _():
            loads[2 * g].wait()
            if g == 0:
                loads[1].wait()

        @pl.when(jnp.logical_not(have))
        def _():
            s_tile[:, side] = jnp.zeros((TB, width), BF16)

        @pl.when(have)
        def _():
            off = pl.multiple_of(lax.rem(tile_ref[g * tiles + t] * TB, chunk), 16)
            for n in range(0, width, WIDE):
                cut = slice(n, n + WIDE)
                rows = buf[slot, g, pl.ds(off, TB), : n + WIDE]
                s_tile[:, g * width + n : g * width + n + WIDE] = apply_upper(
                    rows, m_ref, cut
                ).astype(BF16)
            b_tile[...] -= dot16(s_tile[:, side], lead[g], NT)

    @pl.when(t == 0)
    def _():
        loads[3].wait()

    b_hi, b_lo = split(b_tile[...])

    def panel(n):
        end = n + WIDE
        hi, lo = pivot[0, :end, n:end], pivot[1, :end, n:end]
        return dot16(b_hi[:, :end], hi) + dot16(b_hi[:, :end], lo) + dot16(b_lo[:, :end], hi)

    first = flag_ref[0] != 0
    lead_tile = (flag_ref[1] != 0) & (t < across + width // TB)
    below = t >= across

    @pl.when(jnp.logical_not(below))
    def _():
        here = pl.ds(pl.multiple_of(t * TB, TB), TB)
        s_keep[here, :] = s_tile[...]
        for n in range(0, width, WIDE):
            f_keep[here, n : n + WIDE] = panel(n).astype(BF16)

    @pl.when(below & first & lead_tile)
    def _():
        out_ref[...] = l_ref[...]

    @pl.when(below & first & jnp.logical_not(lead_tile))
    def _():
        for n in range(0, width, WIDE):
            out_ref[:, n : n + WIDE] = panel(n)

    @pl.when(below & jnp.logical_not(first) & lead_tile)
    def _():
        out_ref[...] = jnp.zeros_like(out_ref)

    @pl.when(below & jnp.logical_not(first) & jnp.logical_not(lead_tile))
    def _():
        f = jnp.concatenate([panel(n).astype(BF16) for n in range(0, width, WIDE)], axis=1)
        out_ref[...] = parent_ref[...].astype(F32) - (
            dot16(s_tile[...], s_keep[...], NT) + dot16(f, f_keep[...], NT)
        )


def finish(tiles, have, flags, gathered, m_own, m_far, lead_both, m_pivot, factor, panel, stripe, parent):
    chunk = gathered.shape[2]
    width = lead_both.shape[-1]
    cols = parent.shape[1]
    across = cols // TB
    lead = width // TB
    grid = across + parent.shape[0] // TB
    hbm = pl.BlockSpec(memory_space=pl.ANY)
    pair = VM((2, width, width), BF16)
    stripe_at = lambda t, *_: (jnp.maximum(t - across, 0), 0)
    return pl.pallas_call(
        functools.partial(finish_kernel, chunk, across),
        grid_spec=pltpu.PrefetchScalarGridSpec(
            num_scalar_prefetch=3,
            grid=(grid,),
            in_specs=[
                hbm,
                hbm,
                hbm,
                hbm,
                hbm,
                pl.BlockSpec((TB, width), lambda t, *_: (jnp.clip(t - across, 0, lead - 1), 0)),
                pl.BlockSpec((width, TB), lambda t, *_: (0, jnp.minimum(t, across - 1))),
                pl.BlockSpec((TB, width), stripe_at),
                pl.BlockSpec((TB, cols), stripe_at),
            ],
            out_specs=pl.BlockSpec((TB, cols), stripe_at),
            scratch_shapes=[
                VM((2, 2, chunk_span(chunk) * chunk, width), BF16),
                pltpu.SemaphoreType.DMA((2, 2, chunk_span(chunk))),
                pair,
                pair,
                pair,
                pair,
                pltpu.SemaphoreType.DMA((4,)),
                VM((TB, 2 * width), BF16),
                VM((TB, width), F32),
                VM((cols, 2 * width), BF16),
                VM((cols, width), BF16),
            ],
        ),
        out_shape=jax.ShapeDtypeStruct(parent.shape, F32),
        compiler_params=pltpu.CompilerParams(vmem_limit_bytes=56 * 2**20),
        cost_estimate=pl.CostEstimate(
            flops=60_000_000_000, bytes_accessed=60 * 2**20, transcendentals=0
        ),
        name="finish",
    )(tiles, have, flags, gathered, m_own, m_far, lead_both, m_pivot, factor, panel, stripe, parent)


def locate(tile_map, parent_tiles):
    matches = tile_map[:, None] == jnp.arange(parent_tiles, dtype=jnp.int32)[None, :]
    positions = jnp.arange(tile_map.shape[0], dtype=jnp.int32)[:, None]
    return jnp.sum(jnp.where(matches, positions, 0), axis=0), jnp.any(matches, axis=0)


def per_device(child_update, child_pivot, child_map, parent_front):
    width = child_pivot.shape[-1]
    stripe_rows, block_cols = parent_front.shape
    row_tiles = stripe_rows // TB
    col_tiles = block_cols // TB
    parent_tiles = row_tiles * lax.axis_size("row")
    row = lax.axis_index("row")
    block = lax.axis_index(("grp", "col"))
    raw = child_update[0]
    chunk = raw.shape[0]

    grp = lax.axis_index("grp")
    own_map = jnp.where(grp == 0, child_map, child_map[::-1])
    lead_tiles = jnp.arange(width // TB, dtype=jnp.int32)
    keep = (own_map[0, : width // TB] == lead_tiles).astype(F32)
    keep = jnp.broadcast_to(jnp.repeat(keep, TB)[:, None], (width, 128))
    m_own, m_pivot, pivot_factor, gathered, column_panel, stripe, lead_both, m_far = front(
        child_pivot[0], keep, raw, parent_front
    )
    gathered = gathered.reshape(2, -1, chunk, width)

    wanted_tiles = jnp.concatenate(
        [
            block * col_tiles + jnp.arange(col_tiles, dtype=jnp.int32),
            row * row_tiles + jnp.arange(row_tiles, dtype=jnp.int32),
        ]
    )
    tiles, have = [], []
    for g in range(2):
        inverse, present = locate(own_map[g], parent_tiles)
        tiles.append(inverse[wanted_tiles])
        have.append(present[wanted_tiles].astype(jnp.int32))
    tiles, have = jnp.concatenate(tiles), jnp.concatenate(have)
    flags = jnp.stack([block == 0, row == 0, grp == 1]).astype(jnp.int32)
    return finish(
        tiles, have, flags, gathered, m_own, m_far, lead_both, m_pivot, pivot_factor,
        column_panel, stripe, parent_front,
    )


def solution(mesh):
    in_specs = (P("grp", ("row", "col"), None), P("grp", None, None), P(), P("row", ("grp", "col")))
    out_specs = P("row", ("grp", "col"))
    return jax.shard_map(
        per_device, mesh=mesh, in_specs=in_specs, out_specs=out_specs, check_vma=False
    )
```

```python
import functools

import jax
import jax.numpy as jnp
from jax import lax
from jax.experimental import pallas as pl
from jax.experimental.pallas import tpu as pltpu
from jax.sharding import PartitionSpec as P

TB = 512
F32 = jnp.float32
BF16 = jnp.bfloat16
NB = 128
SUBS = 8
VM = pltpu.VMEM
NT = (((1,), (1,)), ((), ()))
NN = (((1,), (0,)), ((), ()))


CUT = 256
WIDE = 512


def dot16(a, b, dims=NN):
    return lax.dot_general(a, b, dims, preferred_element_type=F32)


def split(x):
    hi = x.astype(BF16)
    return hi, (x - hi.astype(F32)).astype(BF16)


def dot3(a, b):
    ah, al = split(a)
    bh, bl = split(b)
    return dot16(
        jnp.concatenate([ah, ah, al], axis=1), jnp.concatenate([bh, bl, bh], axis=1), NT
    )


def sum_products(x, y):
    terms = [a * b for a, b in zip(x, y)]
    while len(terms) > 1:
        paired = [terms[i] + terms[i + 1] for i in range(0, len(terms) - 1, 2)]
        terms = paired + ([terms[-1]] if len(terms) % 2 else [])
    return terms[0]


class Block:
    def __init__(self, p):
        self.n = len(p)
        if self.n == 2:
            a, b, c = p[0][0], p[1][0], p[1][1]
            det = a * c - b * b
            q = 1.0 / det
            self.entries = (a, b, det)
            self.inverse = (c * q, -b * q, a * q)
            return
        h = self.n // 2
        self.first = Block([row[:h] for row in p[:h]])
        below = [[p[h + x][y] for y in range(h)] for x in range(h)]
        self.gain = [self.first.solve(row) for row in below]
        self.second = Block(
            [
                [p[h + x][h + y] - sum_products(self.gain[x], below[y]) for y in range(x + 1)]
                for x in range(h)
            ]
        )

    def reduce(self, rows):
        h = self.n // 2
        return [rows[h + x] - sum_products(self.gain[x], rows[:h]) for x in range(h)]

    def solve(self, rows):
        if self.n == 2:
            i00, i01, i11 = self.inverse
            return [i00 * rows[0] + i01 * rows[1], i01 * rows[0] + i11 * rows[1]]
        h = self.n // 2
        top = self.first.solve(rows[:h])
        bottom = self.second.solve(self.reduce(rows))
        top = [
            top[y] - sum_products([self.gain[x][y] for x in range(h)], bottom) for y in range(h)
        ]
        return top + bottom

    def half_solve(self, rows):
        if self.n == 2:
            a, b, det = self.entries
            scale = lax.rsqrt(a)
            inv_a = scale * scale
            return [
                rows[0] * scale,
                (rows[1] - (b * inv_a) * rows[0]) * lax.rsqrt(det * inv_a),
            ]
        return self.first.half_solve(rows[: self.n // 2]) + self.second.half_solve(
            self.reduce(rows)
        )


def factor_diagonal(tiles):
    tiles = list(tiles)
    lanes = lax.broadcasted_iota(jnp.int32, (8, 128), 1)
    subs = lax.broadcasted_iota(jnp.int32, (8, 128), 0)
    upper, inverse = [], []
    for v in range(16):
        j = 8 * v
        inside = (lanes >= j) & (lanes < j + SUBS)
        cols = [
            {i: jnp.broadcast_to(tiles[i][:, j + k : j + k + 1], (8, 128)) for i in range(v, 16)}
            for k in range(SUBS)
        ]
        rows = [jnp.broadcast_to(tiles[v][k : k + 1, :], (8, 128)) for k in range(SUBS)]
        pivots = [
            [jnp.broadcast_to(cols[l][v][k : k + 1, :], (8, 128)) for l in range(k + 1)]
            for k in range(SUBS)
        ]
        unit_rows = [
            jnp.where(inside, jnp.where(lanes == j + k, F32(1), F32(0)), rows[k])
            for k in range(SUBS)
        ]
        block = Block(pivots)
        solved = block.solve(unit_rows)
        up, inv = block.half_solve(rows), block.half_solve(unit_rows)
        up_tile, inv_tile = up[0], inv[0]
        for k in range(1, SUBS):
            up_tile = jnp.where(subs == k, up[k], up_tile)
            inv_tile = jnp.where(subs == k, inv[k], inv_tile)
        upper.append(jnp.where(lanes >= subs + j, up_tile, F32(0)))
        inverse.append(jnp.where(lanes <= subs + j, inv_tile, F32(0)))
        for i in range(v + 1, 16):
            tiles[i] = jnp.where(inside, F32(0), tiles[i]) - sum_products(
                [cols[k][i] for k in range(SUBS)], solved
            )
    return upper, inverse


AXES = ("x", "y", "z")
CUTS = ((0, 48), (48, 32), (80, 32))
ORDERS = (("y", "z", "x"), ("z", "x", "y"), ("x", "y", "z"))
LINKS = 144


class Mover:
    def __init__(self, send_sems, recv_sems):
        self.send_sems, self.recv_sems = send_sems, recv_sems
        row, col, grp = lax.axis_index("row"), lax.axis_index("col"), lax.axis_index("grp")
        self.row = row
        self.core = lax.rem(row, 2)
        self.at = {"x": row // 2, "y": grp * 2 + col // 4, "z": lax.rem(col, 4)}
        self.count = 0
        self.sent = []

    def device(self, axis, place):
        if axis == "x":
            return {"row": place * 2 + self.core}
        if axis == "y":
            return {"grp": place // 2, "col": lax.rem(place, 2) * 4 + self.at["z"]}
        return {"col": (self.at["y"] - self.at["y"] // 2 * 2) * 4 + place}

    def sibling(self):
        return {"row": self.row + 1 - 2 * self.core}

    def shifted(self, axis, by):
        return lax.rem(self.at[axis] + (by + 4), 4)

    def greet(self):
        barrier = pltpu.get_barrier_semaphore()
        others = [self.sibling()]
        for axis in AXES:
            others += [self.device(axis, self.shifted(axis, by)) for by in (1, 2, 3)]
        for other in others:
            pl.semaphore_signal(
                barrier, inc=1, device_id=other, device_id_type=pl.DeviceIdType.MESH
            )
        pl.semaphore_wait(barrier, len(others))

    def make(self, src, dst, device, send=True):
        i = self.count
        self.count += 1
        copy = pltpu.make_async_remote_copy(
            src_ref=src,
            dst_ref=dst,
            send_sem=self.send_sems.at[i],
            recv_sem=self.recv_sems.at[i],
            device_id=device,
            device_id_type=pl.DeviceIdType.MESH,
        )
        return copy

    def ring(self, axis, region, when=None):
        here = self.at[axis]
        ahead, behind = self.shifted(axis, 1), self.shifted(axis, -1)
        toward = lax.rem(here + 1 + 2 * self.core, 4)
        away = lax.rem(here + 3 - 2 * self.core, 4)
        plus = self.make(region(here), region(here), self.device(axis, ahead))
        minus = self.make(region(here), region(here), self.device(axis, behind))
        passed = self.make(region(away), region(away), self.device(axis, toward))
        self.sent += [(c, when) for c in (plus, minus, passed)]

        def first():
            plus.start()
            minus.start()

        def second():
            plus.wait_recv()
            minus.wait_recv()
            passed.start()

        def third():
            passed.wait_recv()

        return [guard(when, f) for f in (first, second, third)]

    def line(self, axis, region, when=None):
        here = self.at[axis]
        copies = [
            self.make(region(here), region(here), self.device(axis, self.shifted(axis, by)))
            for by in (1, 3, 2)
        ]
        self.sent += [(c, when) for c in copies]

        def first():
            for c in copies:
                c.start()

        def second():
            for c in copies:
                c.wait_recv()

        return [guard(when, first), guard(when, second)]

    def scatter(self, axis, source, target, when=None):
        here = self.at[axis]
        root, leaf = here == 0, here != 0
        if when is not None:
            root, leaf = root & when, leaf & when
        i = self.count
        self.count += 3
        recv = self.recv_sems.at[i]
        copies = []
        for k in (1, 2, 3):
            copies.append(
                pltpu.make_async_remote_copy(
                    src_ref=source(k),
                    dst_ref=target(k),
                    send_sem=self.send_sems.at[i + k - 1],
                    recv_sem=recv,
                    device_id=self.device(axis, k),
                    device_id_type=pl.DeviceIdType.MESH,
                )
            )
        self.sent += [(c, root) for c in copies]

        def first():
            for c in copies:
                c.start()

        def second():
            copies[0].wait_recv()

        return [guard(root, first), guard(leaf, second)]

    def push(self, region, when=None, taken=None):
        copy = self.make(region, region, self.sibling())
        self.sent.append((copy, when))
        return guard(when, copy.start), guard(taken, copy.wait_recv)

    def finish(self):
        for copy, when in self.sent:
            guard(when, copy.wait_send)()


def guard(when, f):
    if when is None:
        return f

    def guarded():
        pl.when(when)(f)

    return guarded


def merge(*steps):
    def run():
        for s in steps:
            s()

    return run


def rows_of(ref, start, count, cols=None):
    start = pl.multiple_of(start, 16)
    if cols is None:
        return ref.at[pl.ds(start, count)]
    return ref.at[pl.ds(start, count), pl.ds(*cols)]


def gather_program(
    raw, parent, g_ref, d_ref, st_ref, m_ref, u_ref, e_ref, lead, m_far, piece, e_y, e_z, st_a, sems
):
    send_sems, recv_sems, local_sems = sems
    mv = Mover(send_sems, recv_sems)
    x, y, z, core = mv.at["x"], mv.at["y"], mv.at["z"], mv.core
    locals_made = []

    def local(src, dst, when=None):
        copy = pltpu.make_async_copy(src, dst, local_sems.at[len(locals_made)])
        locals_made.append(copy)
        return guard(when, copy.start), guard(when, copy.wait)

    def block(place, cut):
        gy = (place["y"] // 2, lax.rem(place["y"], 2)) if "y" in place else (slice(None),) * 2
        px = place.get("x", slice(None))
        pz = place.get("z", slice(None))
        return g_ref.at[gy[0], px, core, gy[1], pz, pl.ds(*cut)]

    own = local(raw, g_ref.at[y // 2, x, core, lax.rem(y, 2), z])
    a_lists = []
    for cut, order in zip(CUTS, ORDERS):
        place = dict(mv.at)
        steps = []
        for stage, axis in enumerate(order):
            ring = mv.ring(axis, lambda k, p=dict(place), a=axis: block({**p, a: k}, cut))
            if stage == 2:
                base = mv.push(block(place, cut))
                near = [mv.push(block({**place, axis: mv.shifted(axis, by)}, cut)) for by in (1, 3)]
                far = mv.push(block({**place, axis: mv.shifted(axis, 2)}, cut))
                ring[0] = merge(ring[0], base[0])
                ring[1] = merge(ring[1], near[0][0], near[1][0])
                ring[2] = merge(ring[2], far[0])
                ring.append(merge(base[1], near[0][1], near[1][1], far[1]))
            steps += ring
            del place[axis]
        a_lists.append(steps)

    lead_core = core == 0
    part_d = lambda k: rows_of(d_ref, k * 256, 256)
    d_root = local(parent.at[pl.ds(0, 256)], d_ref.at[pl.ds(0, 256)], lead_core & (x == 0))
    hand = mv.scatter("x", lambda k: rows_of(parent, k * 256, 256), part_d, lead_core)
    turn = mv.ring("x", part_d, lead_core)
    push = mv.push(d_ref, lead_core, core == 1)
    d_steps = [
        merge(d_root[0], hand[0]),
        merge(d_root[1], hand[1], turn[0]),
        turn[1],
        merge(turn[2], push[0]),
        push[1],
    ]

    cut_z = lambda k: rows_of(e_ref, y * 256 + k * 64, 64)
    cut_y = lambda k: rows_of(e_ref, k * 256, 256)
    on_y = lead_core & (x == 0) & (z == 0)
    on_z = lead_core & (x == 0)
    loc_y = local(parent.at[pl.ds(0, 256)], e_y, on_y & (y == 0))
    loc_z = local(e_y.at[pl.ds(0, 64)], e_z, on_z & (z == 0))
    loc_x = local(e_z, cut_z(z), on_z)
    hand_y = mv.scatter("y", lambda k: rows_of(parent, k * 256, 256), lambda k: e_y, on_y)
    hand_z = mv.scatter("z", lambda k: e_y.at[pl.ds(64 * k, 64)], lambda k: e_z, on_z)
    hand_x = mv.scatter("x", lambda k: e_z, lambda k: cut_z(z), lead_core)
    turn_z = mv.line("z", cut_z, lead_core)
    turn_y = mv.line("y", cut_y, lead_core)
    push = mv.push(e_ref, lead_core, core == 1)
    e_steps = [
        merge(loc_y[0], hand_y[0]),
        merge(loc_y[1], hand_y[1], loc_z[0], hand_z[0]),
        merge(loc_z[1], hand_z[1], loc_x[0], hand_x[0]),
        merge(loc_x[1], hand_x[1], turn_z[0]),
        merge(turn_z[1], turn_y[0]),
        merge(turn_y[1], push[0]),
        push[1],
    ]

    st_lists = []
    for i, (a, b) in enumerate((("z", "y"), ("y", "z"))):
        wide = lambda k, i=i: rows_of(st_ref, k * 512 + i * 256, 256)
        wide_source = lambda k, i=i: rows_of(parent, k * 512 + i * 256, 256)
        fine = lambda k, a=a, i=i: rows_of(st_ref, mv.at[a] * 512 + i * 256 + k * 64, 64)
        held = st_a.at[i]
        line = mv.at[b] == 0
        loc_a = local(wide_source(0), held, line & (mv.at[a] == 0))
        loc_b = local(held.at[pl.ds(0, 64)], fine(0), line)
        hand_a = mv.scatter(a, wide_source, lambda k: held, line)
        hand_b = mv.scatter(b, lambda k: held.at[pl.ds(k * 64, 64)], fine)
        turn_b = mv.ring(b, fine)
        turn_a = mv.ring(a, wide)
        st_lists.append(
            [
                merge(loc_a[0], hand_a[0]),
                merge(loc_a[1], hand_a[1], loc_b[0], hand_b[0]),
                merge(loc_b[1], hand_b[1], turn_b[0]),
                turn_b[1],
                merge(turn_b[2], turn_a[0]),
                turn_a[1],
                turn_a[2],
            ]
        )

    y_lo = lax.rem(y, 2)
    base = core * (2 * 4 * raw.shape[0])
    size = raw.shape[0]
    chunk_z = lambda k: rows_of(u_ref, base + (y_lo * 4 + k) * size, size)
    u_own = local(raw, chunk_z(z), x == 0)
    u_hand = mv.scatter("x", lambda k: raw, lambda k: chunk_z(z))
    u_turn = mv.line("z", chunk_z)
    full = 8 * size
    rest = e_ref.shape[0] - full
    beside = {"col": (1 - y_lo) * 4 + z}
    half = rows_of(u_ref, y_lo * 4 * size, 4 * size)
    swap = mv.make(half, half, beside)
    mv.sent.append((swap, lead_core))
    tail = u_ref.at[pl.ds(full, rest)]
    slide = mv.make(tail, tail, beside)
    mv.sent.append((slide, (core == 1) & (y_lo == 0)))
    push_head = mv.push(u_ref.at[pl.ds(0, full)], lead_core, core == 1)
    push_tail = mv.push(tail, core == 1, lead_core)
    u_steps = [
        merge(u_own[0], u_hand[0]),
        merge(u_own[1], u_hand[1], u_turn[0]),
        merge(
            u_turn[1],
            guard(lead_core, swap.start),
            guard((core == 1) & (y_lo == 0), slide.start),
        ),
        merge(
            guard(lead_core, swap.wait_recv),
            guard((core == 1) & (y_lo == 1), slide.wait_recv),
            push_head[0],
            push_tail[0],
        ),
        merge(push_head[1], push_tail[1]),
    ]

    def exchange(mine, theirs, direct):
        start = core * 512 + x * 128 + z * 32
        across = mv.make(mine(start, 32), theirs(start, 32), mv.device("y", mv.shifted("y", 2)))
        mv.sent.append((across, None))
        turn = mv.line if direct else mv.ring
        turn_z = turn("z", lambda k: theirs(core * 512 + x * 128 + k * 32, 32))
        turn_x = turn("x", lambda k: theirs(core * 512 + k * 128, 128))
        push = [
            mv.push(theirs(core * 512 + mv.shifted("x", by) * 128, 128)) for by in (0, 1, 3, 2)
        ]
        if direct:
            return [
                across.start,
                merge(across.wait_recv, turn_z[0]),
                merge(turn_z[1], turn_x[0], push[0][0]),
                merge(turn_x[1], push[1][0], push[2][0], push[3][0]),
                merge(*[p[1] for p in push]),
            ]
        return [
            across.start,
            merge(across.wait_recv, turn_z[0]),
            turn_z[1],
            merge(turn_z[2], turn_x[0], push[0][0]),
            merge(turn_x[1], push[1][0], push[2][0]),
            merge(turn_x[2], push[3][0]),
            merge(*[p[1] for p in push]),
        ]

    def part(ref, *lead_index):
        return lambda start, n: ref.at[lead_index + (pl.ds(pl.multiple_of(start, 16), n),)]

    x_steps = exchange(lambda start, n: piece, part(lead, 1), True)
    m_steps = exchange(part(m_ref, slice(None)), part(m_far, slice(None)), False)
    assert mv.count <= LINKS
    a, st = [[merge(*s) for s in zip(*lists)] for lists in (a_lists, st_lists)]
    d, e, u, m = d_steps, e_steps, u_steps, m_steps
    early = [
        merge(mv.greet, own[0], u[0], e[0], own[1]),
        a[0],
        None,
        None,
        None,
        merge(u[1], e[1]),
        a[1],
        e[2],
        merge(a[2], a[3]),
        e[3],
        u[2],
        merge(e[4], st[0]),
        a[4],
        d[0],
        merge(u[3], a[5]),
        merge(e[5], u[4]),
    ]
    late = [
        merge(st[1], a[6]),
        m[0],
        d[1],
        st[2],
        m[1],
        st[3],
        merge(m[2], d[2]),
        st[4],
        m[3],
        d[3],
        a[7],
        None,
        m[4],
        st[5],
        a[8],
        m[5],
    ]
    last = [d[4], st[6], m[6], a[9]]
    return mv, early, x_steps, e[6], late, last


def factor_loop(w, inv_s, up_s, left, right, l_ref, ticks):
    width = w.shape[0]
    steps = width // NB
    if l_ref is not None:
        l_ref[...] = jnp.zeros_like(l_ref)

    def step(k, _):
        o = pl.multiple_of(k * NB, NB)
        here = pl.ds(o, NB)
        for i in range(0, len(ticks), 2):
            if ticks[i] is not None:
                pl.when(k == i // 2)(ticks[i])
        groups = [w[pl.ds(pl.multiple_of(o + 8 * i, 8), 8), here] for i in range(NB // 8)]
        up, inv = factor_diagonal(groups)
        for i in range(NB // 8):
            inv_s[8 * i : 8 * i + 8, :] = inv[i]
            up_s[8 * i : 8 * i + 8, :] = up[i]
        inverse = inv_s[...]
        panel = dot3(w[:, here], inverse)

        def clear(j, _):
            w[here, pl.ds(pl.multiple_of(j * NB, NB), NB)] = jnp.zeros((NB, NB), F32)
            return 0

        lax.fori_loop(k + 1, steps, clear, 0)
        w[:, here] = panel
        w[here, here] = inverse.T
        hi, lo = split(w[:, here])
        left[:, :NB] = hi
        left[:, NB : 2 * NB] = hi
        left[:, 2 * NB :] = lo
        right[:, :NB] = hi
        right[:, NB : 2 * NB] = lo
        right[:, 2 * NB :] = hi
        right[here, :] = jnp.zeros((NB, 3 * NB), BF16)
        if l_ref is not None:
            l_ref[here, here] = up_s[...].T

            def keep(j, _):
                below = pl.ds(pl.multiple_of(j * NB, NB), NB)
                l_ref[below, here] = w[below, here]
                return 0

            lax.fori_loop(k + 1, steps, keep, 0)
        for i in range(1, len(ticks), 2):
            if ticks[i] is not None:
                pl.when(k == i // 2)(ticks[i])

        def update(j, _):
            there = pl.ds(pl.multiple_of(j * CUT, CUT), CUT)
            w[:, there] -= dot16(left[...], right[there, :], NT)
            return 0

        lax.fori_loop((k + 1) * NB // CUT, width // CUT, update, 0)
        return 0

    lax.fori_loop(0, steps, step, 0)


def split_upper(w, m_ref):
    width = w.shape[0]
    for n in range(width // NB):
        cut = slice(n * NB, (n + 1) * NB)
        end = (n + 1) * NB
        hi, lo = split(w[:end, cut])
        m_ref[0, :end, cut] = hi
        m_ref[1, :end, cut] = lo
        if end < width:
            m_ref[:, end:, cut] = jnp.zeros((2, width - end, NB), BF16)


def apply_upper(rows, m_ref, cut):
    return dot16(rows, m_ref[0, : cut.stop, cut]) + dot16(rows, m_ref[1, : cut.stop, cut])


def front_kernel(
    a_ref, keep_ref, raw, parent,
    m_ref, m_pivot, l_ref, g_ref, d_ref, st_ref, lead_out, far_out,
    w, inv_s, up_s, left, right, u_ref, e_ref, lead, m_far, piece, e_y, e_z, st_a,
    send_sems, recv_sems, local_sems,
):
    width = a_ref.shape[0]
    mv, early, swap, pivot_here, late, last = gather_program(
        raw, parent, g_ref, d_ref, st_ref, m_ref, u_ref, e_ref, lead, m_far, piece, e_y, e_z,
        st_a, (send_sems, recv_sems, local_sems),
    )
    cuts = [slice(n, n + CUT) for n in range(0, width, CUT)]
    w[...] = a_ref[...]
    factor_loop(w, inv_s, up_s, left, right, None, early)
    split_upper(w, m_ref)
    mine = pl.ds(pl.multiple_of(mv.core * 512 + mv.at["x"] * 128 + mv.at["z"] * 32, 32), 32)
    for cut in cuts:
        both = apply_upper(u_ref[mine, : cut.stop], m_ref, cut)
        piece[:, cut] = (both * keep_ref[mine, :1]).astype(BF16)
    swap[0]()
    for cut in cuts:
        both = apply_upper(u_ref[:width, : cut.stop], m_ref, cut)
        lead[0, :, cut] = (both * keep_ref[:, :1]).astype(BF16)
    swap[1]()
    pivot_here()

    def subtract(i, cut, total):
        w[cut.start :, cut] = total - dot16(lead[i, cut.start :, :], lead[i, cut, :], NT)

    for n, cut in enumerate(cuts):
        if n == 1:
            swap[2]()
        subtract(0, cut, e_ref[cut.start :, cut].astype(F32))
    for step in swap[3:]:
        step()
    lead_copy = pltpu.make_async_copy(lead, lead_out, local_sems.at[14])
    far_copy = pltpu.make_async_copy(m_far, far_out, local_sems.at[15])
    lead_copy.start()
    for cut in cuts:
        subtract(1, cut, w[cut.start :, cut])
    factor_loop(w, inv_s, up_s, left, right, l_ref, late)
    split_upper(w, m_pivot)
    for step in last[:3]:
        step()
    far_copy.start()
    for step in last[3:]:
        step()
    mv.finish()
    lead_copy.wait()
    far_copy.wait()


def front(block, keep, raw, parent):
    width = block.shape[0]
    chunk = raw.shape[0]
    hbm = pl.BlockSpec(memory_space=pl.ANY)
    vmem = pl.BlockSpec(memory_space=VM)
    pair = jax.ShapeDtypeStruct((2, width, width), BF16)
    return pl.pallas_call(
        front_kernel,
        out_shape=[
            pair,
            pair,
            jax.ShapeDtypeStruct((width, width), F32),
            jax.ShapeDtypeStruct((2, 4, 2, 2, 4, chunk, width), BF16),
            jax.ShapeDtypeStruct((width, width), BF16),
            jax.ShapeDtypeStruct(parent.shape, BF16),
            pair,
            pair,
        ],
        in_specs=[vmem, vmem, hbm, hbm],
        out_specs=[vmem, vmem, vmem, hbm, hbm, hbm, hbm, hbm],
        scratch_shapes=[
            VM((width, width), F32),
            VM((NB, NB), F32),
            VM((NB, NB), F32),
            VM((width, 3 * NB), BF16),
            VM((width, 3 * NB), BF16),
            VM((16 * chunk, width), BF16),
            VM((width, width), BF16),
            VM((2, width, width), BF16),
            VM((2, width, width), BF16),
            VM((32, width), BF16),
            VM((256, width), BF16),
            VM((64, width), BF16),
            VM((2, 256, width), BF16),
            pltpu.SemaphoreType.DMA((LINKS,)),
            pltpu.SemaphoreType.DMA((LINKS,)),
            pltpu.SemaphoreType.DMA((16,)),
        ],
        compiler_params=pltpu.CompilerParams(
            vmem_limit_bytes=52 * 2**20, collective_id=0, has_side_effects=True
        ),
        cost_estimate=pl.CostEstimate(
            flops=120_000_000_000, bytes_accessed=16 * width * width, transcendentals=0
        ),
        name="front",
    )(block, keep, raw, parent)


def chunk_span(chunk):
    return -(-(TB + chunk - 16) // chunk)


def finish_kernel(
    chunk, across, tile_ref, have_ref, flag_ref, gathered, own_hbm, far_hbm, lead_hbm, pivot_hbm,
    l_ref, d_ref, st_ref, parent_ref, out_ref,
    buf, sem, own, far, lead, pivot, load_sem, s_tile, b_tile, s_keep, f_keep,
):
    t = pl.program_id(0)
    tiles = pl.num_programs(0)
    width = b_tile.shape[1]
    span = chunk_span(chunk)
    slot = lax.rem(t, 2)

    def copies(t, slot):
        out = []
        for g in range(2):
            first = tile_ref[g * tiles + t] * TB // chunk
            for i in range(span):
                c = jnp.minimum(first + i, gathered.shape[1] - 1)
                out.append(
                    pltpu.make_async_copy(
                        gathered.at[g ^ flag_ref[2], c],
                        buf.at[slot, g, pl.ds(i * chunk, chunk)],
                        sem.at[slot, g, i],
                    )
                )
        return out

    loads = [
        pltpu.make_async_copy(src, dst, load_sem.at[i])
        for i, (src, dst) in enumerate(
            ((own_hbm, own), (lead_hbm, lead), (far_hbm, far), (pivot_hbm, pivot))
        )
    ]

    @pl.when(t == 0)
    def _():
        for c in copies(t, slot):
            c.start()
        for c in loads:
            c.start()

    @pl.when(t + 1 < tiles)
    def _():
        for c in copies(t + 1, 1 - slot):
            c.start()

    for c in copies(t, slot):
        c.wait()

    @pl.when(t < across)
    def _():
        b_tile[...] = d_ref[...].astype(F32).T

    @pl.when(t >= across)
    def _():
        b_tile[...] = st_ref[...].astype(F32)

    for g, m_ref in enumerate((own, far)):
        have = have_ref[g * tiles + t] != 0
        side = slice(g * width, (g + 1) * width)

        @pl.when(t == 0)
        def _():
            loads[2 * g].wait()
            if g == 0:
                loads[1].wait()

        @pl.when(jnp.logical_not(have))
        def _():
            s_tile[:, side] = jnp.zeros((TB, width), BF16)

        @pl.when(have)
        def _():
            off = pl.multiple_of(lax.rem(tile_ref[g * tiles + t] * TB, chunk), 16)
            for n in range(0, width, WIDE):
                cut = slice(n, n + WIDE)
                rows = buf[slot, g, pl.ds(off, TB), : n + WIDE]
                s_tile[:, g * width + n : g * width + n + WIDE] = apply_upper(
                    rows, m_ref, cut
                ).astype(BF16)
            b_tile[...] -= dot16(s_tile[:, side], lead[g], NT)

    @pl.when(t == 0)
    def _():
        loads[3].wait()

    b_hi, b_lo = split(b_tile[...])

    def panel(n):
        end = n + WIDE
        hi, lo = pivot[0, :end, n:end], pivot[1, :end, n:end]
        return dot16(b_hi[:, :end], hi) + dot16(b_hi[:, :end], lo) + dot16(b_lo[:, :end], hi)

    first = flag_ref[0] != 0
    lead_tile = (flag_ref[1] != 0) & (t < across + width // TB)
    below = t >= across

    @pl.when(jnp.logical_not(below))
    def _():
        here = pl.ds(pl.multiple_of(t * TB, TB), TB)
        s_keep[here, :] = s_tile[...]
        for n in range(0, width, WIDE):
            f_keep[here, n : n + WIDE] = panel(n).astype(BF16)

    @pl.when(below & first & lead_tile)
    def _():
        out_ref[...] = l_ref[...]

    @pl.when(below & first & jnp.logical_not(lead_tile))
    def _():
        for n in range(0, width, WIDE):
            out_ref[:, n : n + WIDE] = panel(n)

    @pl.when(below & jnp.logical_not(first) & lead_tile)
    def _():
        out_ref[...] = jnp.zeros_like(out_ref)

    @pl.when(below & jnp.logical_not(first) & jnp.logical_not(lead_tile))
    def _():
        f = jnp.concatenate([panel(n).astype(BF16) for n in range(0, width, WIDE)], axis=1)
        out_ref[...] = parent_ref[...].astype(F32) - (
            dot16(s_tile[...], s_keep[...], NT) + dot16(f, f_keep[...], NT)
        )


def finish(tiles, have, flags, gathered, m_own, m_far, lead_both, m_pivot, factor, panel, stripe, parent):
    chunk = gathered.shape[2]
    width = lead_both.shape[-1]
    cols = parent.shape[1]
    across = cols // TB
    lead = width // TB
    grid = across + parent.shape[0] // TB
    hbm = pl.BlockSpec(memory_space=pl.ANY)
    pair = VM((2, width, width), BF16)
    stripe_at = lambda t, *_: (jnp.maximum(t - across, 0), 0)
    return pl.pallas_call(
        functools.partial(finish_kernel, chunk, across),
        grid_spec=pltpu.PrefetchScalarGridSpec(
            num_scalar_prefetch=3,
            grid=(grid,),
            in_specs=[
                hbm,
                hbm,
                hbm,
                hbm,
                hbm,
                pl.BlockSpec((TB, width), lambda t, *_: (jnp.clip(t - across, 0, lead - 1), 0)),
                pl.BlockSpec((width, TB), lambda t, *_: (0, jnp.minimum(t, across - 1))),
                pl.BlockSpec((TB, width), stripe_at),
                pl.BlockSpec((TB, cols), stripe_at),
            ],
            out_specs=pl.BlockSpec((TB, cols), stripe_at),
            scratch_shapes=[
                VM((2, 2, chunk_span(chunk) * chunk, width), BF16),
                pltpu.SemaphoreType.DMA((2, 2, chunk_span(chunk))),
                pair,
                pair,
                pair,
                pair,
                pltpu.SemaphoreType.DMA((4,)),
                VM((TB, 2 * width), BF16),
                VM((TB, width), F32),
                VM((cols, 2 * width), BF16),
                VM((cols, width), BF16),
            ],
        ),
        out_shape=jax.ShapeDtypeStruct(parent.shape, F32),
        compiler_params=pltpu.CompilerParams(vmem_limit_bytes=56 * 2**20),
        cost_estimate=pl.CostEstimate(
            flops=60_000_000_000, bytes_accessed=60 * 2**20, transcendentals=0
        ),
        name="finish",
    )(tiles, have, flags, gathered, m_own, m_far, lead_both, m_pivot, factor, panel, stripe, parent)


def locate(tile_map, parent_tiles):
    matches = tile_map[:, None] == jnp.arange(parent_tiles, dtype=jnp.int32)[None, :]
    positions = jnp.arange(tile_map.shape[0], dtype=jnp.int32)[:, None]
    return jnp.sum(jnp.where(matches, positions, 0), axis=0), jnp.any(matches, axis=0)


def per_device(child_update, child_pivot, child_map, parent_front):
    width = child_pivot.shape[-1]
    stripe_rows, block_cols = parent_front.shape
    row_tiles = stripe_rows // TB
    col_tiles = block_cols // TB
    parent_tiles = row_tiles * lax.axis_size("row")
    row = lax.axis_index("row")
    block = lax.axis_index(("grp", "col"))
    raw = child_update[0]
    chunk = raw.shape[0]

    grp = lax.axis_index("grp")
    own_map = jnp.where(grp == 0, child_map, child_map[::-1])
    lead_tiles = jnp.arange(width // TB, dtype=jnp.int32)
    keep = (own_map[0, : width // TB] == lead_tiles).astype(F32)
    keep = jnp.broadcast_to(jnp.repeat(keep, TB)[:, None], (width, 128))
    m_own, m_pivot, pivot_factor, gathered, column_panel, stripe, lead_both, m_far = front(
        child_pivot[0], keep, raw, parent_front
    )
    gathered = gathered.reshape(2, -1, chunk, width)

    wanted_tiles = jnp.concatenate(
        [
            block * col_tiles + jnp.arange(col_tiles, dtype=jnp.int32),
            row * row_tiles + jnp.arange(row_tiles, dtype=jnp.int32),
        ]
    )
    tiles, have = [], []
    for g in range(2):
        inverse, present = locate(own_map[g], parent_tiles)
        tiles.append(inverse[wanted_tiles])
        have.append(present[wanted_tiles].astype(jnp.int32))
    tiles, have = jnp.concatenate(tiles), jnp.concatenate(have)
    flags = jnp.stack([block == 0, row == 0, grp == 1]).astype(jnp.int32)
    return finish(
        tiles, have, flags, gathered, m_own, m_far, lead_both, m_pivot, pivot_factor,
        column_panel, stripe, parent_front,
    )


def solution(mesh):
    in_specs = (P("grp", ("row", "col"), None), P("grp", None, None), P(), P("row", ("grp", "col")))
    out_specs = P("row", ("grp", "col"))
    return jax.shard_map(
        per_device, mesh=mesh, in_specs=in_specs, out_specs=out_specs, check_vma=False
    )
```

```python
import functools

import jax
import jax.numpy as jnp
from jax import lax
from jax.experimental import pallas as pl
from jax.experimental.pallas import tpu as pltpu
from jax.sharding import PartitionSpec as P

TB = 512
F32 = jnp.float32
BF16 = jnp.bfloat16
NB = 128
SUBS = 8
VM = pltpu.VMEM
NT = (((1,), (1,)), ((), ()))
NN = (((1,), (0,)), ((), ()))


CUT = 256
WIDE = 512


def dot16(a, b, dims=NN):
    return lax.dot_general(a, b, dims, preferred_element_type=F32)


def split(x):
    hi = x.astype(BF16)
    return hi, (x - hi.astype(F32)).astype(BF16)


def dot3(a, b):
    ah, al = split(a)
    bh, bl = split(b)
    return dot16(
        jnp.concatenate([ah, ah, al], axis=1), jnp.concatenate([bh, bl, bh], axis=1), NT
    )


def sum_products(x, y):
    terms = [a * b for a, b in zip(x, y)]
    while len(terms) > 1:
        paired = [terms[i] + terms[i + 1] for i in range(0, len(terms) - 1, 2)]
        terms = paired + ([terms[-1]] if len(terms) % 2 else [])
    return terms[0]


class Block:
    def __init__(self, p):
        self.n = len(p)
        if self.n == 2:
            a, b, c = p[0][0], p[1][0], p[1][1]
            det = a * c - b * b
            q = 1.0 / det
            self.entries = (a, b, det)
            self.inverse = (c * q, -b * q, a * q)
            return
        h = self.n // 2
        self.first = Block([row[:h] for row in p[:h]])
        below = [[p[h + x][y] for y in range(h)] for x in range(h)]
        self.gain = [self.first.solve(row) for row in below]
        self.second = Block(
            [
                [p[h + x][h + y] - sum_products(self.gain[x], below[y]) for y in range(x + 1)]
                for x in range(h)
            ]
        )

    def reduce(self, rows):
        h = self.n // 2
        return [rows[h + x] - sum_products(self.gain[x], rows[:h]) for x in range(h)]

    def solve(self, rows):
        if self.n == 2:
            i00, i01, i11 = self.inverse
            return [i00 * rows[0] + i01 * rows[1], i01 * rows[0] + i11 * rows[1]]
        h = self.n // 2
        top = self.first.solve(rows[:h])
        bottom = self.second.solve(self.reduce(rows))
        top = [
            top[y] - sum_products([self.gain[x][y] for x in range(h)], bottom) for y in range(h)
        ]
        return top + bottom

    def half_solve(self, rows):
        if self.n == 2:
            a, b, det = self.entries
            scale = lax.rsqrt(a)
            inv_a = scale * scale
            return [
                rows[0] * scale,
                (rows[1] - (b * inv_a) * rows[0]) * lax.rsqrt(det * inv_a),
            ]
        return self.first.half_solve(rows[: self.n // 2]) + self.second.half_solve(
            self.reduce(rows)
        )


def factor_diagonal(tiles):
    tiles = list(tiles)
    lanes = lax.broadcasted_iota(jnp.int32, (8, 128), 1)
    subs = lax.broadcasted_iota(jnp.int32, (8, 128), 0)
    upper, inverse = [], []
    for v in range(16):
        j = 8 * v
        inside = (lanes >= j) & (lanes < j + SUBS)
        cols = [
            {i: jnp.broadcast_to(tiles[i][:, j + k : j + k + 1], (8, 128)) for i in range(v, 16)}
            for k in range(SUBS)
        ]
        rows = [jnp.broadcast_to(tiles[v][k : k + 1, :], (8, 128)) for k in range(SUBS)]
        pivots = [
            [jnp.broadcast_to(cols[l][v][k : k + 1, :], (8, 128)) for l in range(k + 1)]
            for k in range(SUBS)
        ]
        unit_rows = [
            jnp.where(inside, jnp.where(lanes == j + k, F32(1), F32(0)), rows[k])
            for k in range(SUBS)
        ]
        block = Block(pivots)
        solved = block.solve(unit_rows)
        up, inv = block.half_solve(rows), block.half_solve(unit_rows)
        up_tile, inv_tile = up[0], inv[0]
        for k in range(1, SUBS):
            up_tile = jnp.where(subs == k, up[k], up_tile)
            inv_tile = jnp.where(subs == k, inv[k], inv_tile)
        upper.append(jnp.where(lanes >= subs + j, up_tile, F32(0)))
        inverse.append(jnp.where(lanes <= subs + j, inv_tile, F32(0)))
        for i in range(v + 1, 16):
            tiles[i] = jnp.where(inside, F32(0), tiles[i]) - sum_products(
                [cols[k][i] for k in range(SUBS)], solved
            )
    return upper, inverse


AXES = ("x", "y", "z")
CUTS = ((0, 48), (48, 32), (80, 32))
ORDERS = (("y", "z", "x"), ("z", "x", "y"), ("x", "y", "z"))
LINKS = 144


class Mover:
    def __init__(self, send_sems, recv_sems):
        self.send_sems, self.recv_sems = send_sems, recv_sems
        row, col, grp = lax.axis_index("row"), lax.axis_index("col"), lax.axis_index("grp")
        self.row = row
        self.core = lax.rem(row, 2)
        self.at = {"x": row // 2, "y": grp * 2 + col // 4, "z": lax.rem(col, 4)}
        self.count = 0
        self.sent = []

    def device(self, axis, place):
        if axis == "x":
            return {"row": place * 2 + self.core}
        if axis == "y":
            return {"grp": place // 2, "col": lax.rem(place, 2) * 4 + self.at["z"]}
        return {"col": (self.at["y"] - self.at["y"] // 2 * 2) * 4 + place}

    def sibling(self):
        return {"row": self.row + 1 - 2 * self.core}

    def shifted(self, axis, by):
        return lax.rem(self.at[axis] + (by + 4), 4)

    def greet(self):
        barrier = pltpu.get_barrier_semaphore()
        others = [self.sibling()]
        for axis in AXES:
            others += [self.device(axis, self.shifted(axis, by)) for by in (1, 2, 3)]
        for other in others:
            pl.semaphore_signal(
                barrier, inc=1, device_id=other, device_id_type=pl.DeviceIdType.MESH
            )
        pl.semaphore_wait(barrier, len(others))

    def make(self, src, dst, device, send=True):
        i = self.count
        self.count += 1
        copy = pltpu.make_async_remote_copy(
            src_ref=src,
            dst_ref=dst,
            send_sem=self.send_sems.at[i],
            recv_sem=self.recv_sems.at[i],
            device_id=device,
            device_id_type=pl.DeviceIdType.MESH,
        )
        return copy

    def ring(self, axis, region, when=None):
        here = self.at[axis]
        ahead, behind = self.shifted(axis, 1), self.shifted(axis, -1)
        toward = lax.rem(here + 1 + 2 * self.core, 4)
        away = lax.rem(here + 3 - 2 * self.core, 4)
        plus = self.make(region(here), region(here), self.device(axis, ahead))
        minus = self.make(region(here), region(here), self.device(axis, behind))
        passed = self.make(region(away), region(away), self.device(axis, toward))
        self.sent += [(c, when) for c in (plus, minus, passed)]

        def first():
            plus.start()
            minus.start()

        def second():
            plus.wait_recv()
            minus.wait_recv()
            passed.start()

        def third():
            passed.wait_recv()

        return [guard(when, f) for f in (first, second, third)]

    def line(self, axis, region, when=None):
        here = self.at[axis]
        copies = [
            self.make(region(here), region(here), self.device(axis, self.shifted(axis, by)))
            for by in (1, 3, 2)
        ]
        self.sent += [(c, when) for c in copies]

        def first():
            for c in copies:
                c.start()

        def second():
            for c in copies:
                c.wait_recv()

        return [guard(when, first), guard(when, second)]

    def scatter(self, axis, source, target, when=None):
        here = self.at[axis]
        root, leaf = here == 0, here != 0
        if when is not None:
            root, leaf = root & when, leaf & when
        i = self.count
        self.count += 3
        recv = self.recv_sems.at[i]
        copies = []
        for k in (1, 2, 3):
            copies.append(
                pltpu.make_async_remote_copy(
                    src_ref=source(k),
                    dst_ref=target(k),
                    send_sem=self.send_sems.at[i + k - 1],
                    recv_sem=recv,
                    device_id=self.device(axis, k),
                    device_id_type=pl.DeviceIdType.MESH,
                )
            )
        self.sent += [(c, root) for c in copies]

        def first():
            for c in copies:
                c.start()

        def second():
            copies[0].wait_recv()

        return [guard(root, first), guard(leaf, second)]

    def push(self, region, when=None, taken=None):
        copy = self.make(region, region, self.sibling())
        self.sent.append((copy, when))
        return guard(when, copy.start), guard(taken, copy.wait_recv)

    def finish(self):
        for copy, when in self.sent:
            guard(when, copy.wait_send)()


def guard(when, f):
    if when is None:
        return f

    def guarded():
        pl.when(when)(f)

    return guarded


def merge(*steps):
    def run():
        for s in steps:
            s()

    return run


def rows_of(ref, start, count, cols=None):
    start = pl.multiple_of(start, 16)
    if cols is None:
        return ref.at[pl.ds(start, count)]
    return ref.at[pl.ds(start, count), pl.ds(*cols)]


def gather_program(
    raw, parent, g_ref, d_ref, st_ref, m_ref, u_ref, e_ref, lead, m_far, piece, e_y, e_z, st_a, sems
):
    send_sems, recv_sems, local_sems = sems
    mv = Mover(send_sems, recv_sems)
    x, y, z, core = mv.at["x"], mv.at["y"], mv.at["z"], mv.core
    locals_made = []

    def local(src, dst, when=None):
        copy = pltpu.make_async_copy(src, dst, local_sems.at[len(locals_made)])
        locals_made.append(copy)
        return guard(when, copy.start), guard(when, copy.wait)

    def block(place, cut):
        gy = (place["y"] // 2, lax.rem(place["y"], 2)) if "y" in place else (slice(None),) * 2
        px = place.get("x", slice(None))
        pz = place.get("z", slice(None))
        return g_ref.at[gy[0], px, core, gy[1], pz, pl.ds(*cut)]

    own = local(raw, g_ref.at[y // 2, x, core, lax.rem(y, 2), z])
    a_lists = []
    for cut, order in zip(CUTS, ORDERS):
        place = dict(mv.at)
        steps = []
        for stage, axis in enumerate(order):
            ring = mv.ring(axis, lambda k, p=dict(place), a=axis: block({**p, a: k}, cut))
            if stage == 2:
                base = mv.push(block(place, cut))
                near = [mv.push(block({**place, axis: mv.shifted(axis, by)}, cut)) for by in (1, 3)]
                far = mv.push(block({**place, axis: mv.shifted(axis, 2)}, cut))
                ring[0] = merge(ring[0], base[0])
                ring[1] = merge(ring[1], near[0][0], near[1][0])
                ring[2] = merge(ring[2], far[0])
                ring.append(merge(base[1], near[0][1], near[1][1], far[1]))
            steps += ring
            del place[axis]
        a_lists.append(steps)

    lead_core = core == 0
    part_d = lambda k: rows_of(d_ref, k * 256, 256)
    d_root = local(parent.at[pl.ds(0, 256)], d_ref.at[pl.ds(0, 256)], lead_core & (x == 0))
    hand = mv.scatter("x", lambda k: rows_of(parent, k * 256, 256), part_d, lead_core)
    turn = mv.ring("x", part_d, lead_core)
    push = mv.push(d_ref, lead_core, core == 1)
    d_steps = [
        merge(d_root[0], hand[0]),
        merge(d_root[1], hand[1], turn[0]),
        turn[1],
        merge(turn[2], push[0]),
        push[1],
    ]

    cut_z = lambda k: rows_of(e_ref, y * 256 + k * 64, 64)
    cut_y = lambda k: rows_of(e_ref, k * 256, 256)
    on_y = lead_core & (x == 0) & (z == 0)
    on_z = lead_core & (x == 0)
    loc_y = local(parent.at[pl.ds(0, 256)], e_y, on_y & (y == 0))
    loc_z = local(e_y.at[pl.ds(0, 64)], e_z, on_z & (z == 0))
    loc_x = local(e_z, cut_z(z), on_z)
    hand_y = mv.scatter("y", lambda k: rows_of(parent, k * 256, 256), lambda k: e_y, on_y)
    hand_z = mv.scatter("z", lambda k: e_y.at[pl.ds(64 * k, 64)], lambda k: e_z, on_z)
    hand_x = mv.scatter("x", lambda k: e_z, lambda k: cut_z(z), lead_core)
    turn_z = mv.line("z", cut_z, lead_core)
    turn_y = mv.line("y", cut_y, lead_core)
    push = mv.push(e_ref, lead_core, core == 1)
    e_steps = [
        merge(loc_y[0], hand_y[0]),
        merge(loc_y[1], hand_y[1], loc_z[0], hand_z[0]),
        merge(loc_z[1], hand_z[1], loc_x[0], hand_x[0]),
        merge(loc_x[1], hand_x[1], turn_z[0]),
        merge(turn_z[1], turn_y[0]),
        merge(turn_y[1], push[0]),
        push[1],
    ]

    st_lists = []
    for i, (a, b) in enumerate((("z", "y"), ("y", "z"))):
        wide = lambda k, i=i: rows_of(st_ref, k * 512 + i * 256, 256)
        wide_source = lambda k, i=i: rows_of(parent, k * 512 + i * 256, 256)
        fine = lambda k, a=a, i=i: rows_of(st_ref, mv.at[a] * 512 + i * 256 + k * 64, 64)
        held = st_a.at[i]
        line = mv.at[b] == 0
        loc_a = local(wide_source(0), held, line & (mv.at[a] == 0))
        loc_b = local(held.at[pl.ds(0, 64)], fine(0), line)
        hand_a = mv.scatter(a, wide_source, lambda k: held, line)
        hand_b = mv.scatter(b, lambda k: held.at[pl.ds(k * 64, 64)], fine)
        turn_b = mv.ring(b, fine)
        turn_a = mv.ring(a, wide)
        st_lists.append(
            [
                merge(loc_a[0], hand_a[0]),
                merge(loc_a[1], hand_a[1], loc_b[0], hand_b[0]),
                merge(loc_b[1], hand_b[1], turn_b[0]),
                turn_b[1],
                merge(turn_b[2], turn_a[0]),
                turn_a[1],
                turn_a[2],
            ]
        )

    y_lo = lax.rem(y, 2)
    base = core * (2 * 4 * raw.shape[0])
    size = raw.shape[0]
    chunk_z = lambda k: rows_of(u_ref, base + (y_lo * 4 + k) * size, size)
    u_own = local(raw, chunk_z(z), x == 0)
    u_hand = mv.scatter("x", lambda k: raw, lambda k: chunk_z(z))
    u_turn = mv.line("z", chunk_z)
    full = 8 * size
    rest = e_ref.shape[0] - full
    beside = {"col": (1 - y_lo) * 4 + z}
    half = rows_of(u_ref, y_lo * 4 * size, 4 * size)
    swap = mv.make(half, half, beside)
    mv.sent.append((swap, lead_core))
    tail = u_ref.at[pl.ds(full, rest)]
    slide = mv.make(tail, tail, beside)
    mv.sent.append((slide, (core == 1) & (y_lo == 0)))
    push_head = mv.push(u_ref.at[pl.ds(0, full)], lead_core, core == 1)
    push_tail = mv.push(tail, core == 1, lead_core)
    u_steps = [
        merge(u_own[0], u_hand[0]),
        merge(u_own[1], u_hand[1], u_turn[0]),
        merge(
            u_turn[1],
            guard(lead_core, swap.start),
            guard((core == 1) & (y_lo == 0), slide.start),
        ),
        merge(
            guard(lead_core, swap.wait_recv),
            guard((core == 1) & (y_lo == 1), slide.wait_recv),
            push_head[0],
            push_tail[0],
        ),
        merge(push_head[1], push_tail[1]),
    ]

    def exchange(mine, theirs, direct):
        start = core * 512 + x * 128 + z * 32
        across = mv.make(mine(start, 32), theirs(start, 32), mv.device("y", mv.shifted("y", 2)))
        mv.sent.append((across, None))
        turn = mv.line if direct else mv.ring
        turn_z = turn("z", lambda k: theirs(core * 512 + x * 128 + k * 32, 32))
        turn_x = turn("x", lambda k: theirs(core * 512 + k * 128, 128))
        push = [
            mv.push(theirs(core * 512 + mv.shifted("x", by) * 128, 128)) for by in (0, 1, 3, 2)
        ]
        if direct:
            return [
                across.start,
                merge(across.wait_recv, turn_z[0]),
                merge(turn_z[1], turn_x[0], push[0][0]),
                merge(turn_x[1], push[1][0], push[2][0], push[3][0]),
                merge(*[p[1] for p in push]),
            ]
        return [
            across.start,
            merge(across.wait_recv, turn_z[0]),
            turn_z[1],
            merge(turn_z[2], turn_x[0], push[0][0]),
            merge(turn_x[1], push[1][0], push[2][0]),
            merge(turn_x[2], push[3][0]),
            merge(*[p[1] for p in push]),
        ]

    def part(ref, *lead_index):
        return lambda start, n: ref.at[lead_index + (pl.ds(pl.multiple_of(start, 16), n),)]

    x_steps = exchange(lambda start, n: piece, part(lead, 1), True)
    m_steps = exchange(part(m_ref, slice(None)), part(m_far, slice(None)), False)
    assert mv.count <= LINKS
    a, st = [[merge(*s) for s in zip(*lists)] for lists in (a_lists, st_lists)]
    d, e, u, m = d_steps, e_steps, u_steps, m_steps
    early = [
        merge(mv.greet, own[0], u[0], e[0], own[1]),
        a[0],
        None,
        None,
        None,
        merge(u[1], e[1]),
        a[1],
        merge(e[2], st[0]),
        merge(a[2], a[3]),
        e[3],
        u[2],
        merge(e[4], d[0]),
        a[4],
        None,
        merge(u[3], a[5]),
        merge(e[5], u[4], st[1]),
    ]
    late = [
        merge(st[2], a[6]),
        m[0],
        d[1],
        st[3],
        m[1],
        st[4],
        merge(m[2], d[2]),
        None,
        m[3],
        d[3],
        merge(a[7], st[5]),
        None,
        m[4],
        st[6],
        a[8],
        m[5],
    ]
    last = [d[4], m[6], a[9]]
    return mv, early, x_steps, e[6], late, last


def factor_loop(w, inv_s, up_s, left, right, l_ref, ticks):
    width = w.shape[0]
    steps = width // NB
    if l_ref is not None:
        l_ref[...] = jnp.zeros_like(l_ref)

    def step(k, _):
        o = pl.multiple_of(k * NB, NB)
        here = pl.ds(o, NB)
        for i in range(0, len(ticks), 2):
            if ticks[i] is not None:
                pl.when(k == i // 2)(ticks[i])
        groups = [w[pl.ds(pl.multiple_of(o + 8 * i, 8), 8), here] for i in range(NB // 8)]
        up, inv = factor_diagonal(groups)
        for i in range(NB // 8):
            inv_s[8 * i : 8 * i + 8, :] = inv[i]
            up_s[8 * i : 8 * i + 8, :] = up[i]
        inverse = inv_s[...]
        panel = dot3(w[:, here], inverse)

        def clear(j, _):
            w[here, pl.ds(pl.multiple_of(j * NB, NB), NB)] = jnp.zeros((NB, NB), F32)
            return 0

        lax.fori_loop(k + 1, steps, clear, 0)
        w[:, here] = panel
        w[here, here] = inverse.T
        hi, lo = split(w[:, here])
        left[:, :NB] = hi
        left[:, NB : 2 * NB] = hi
        left[:, 2 * NB :] = lo
        right[:, :NB] = hi
        right[:, NB : 2 * NB] = lo
        right[:, 2 * NB :] = hi
        right[here, :] = jnp.zeros((NB, 3 * NB), BF16)
        if l_ref is not None:
            l_ref[here, here] = up_s[...].T

            def keep(j, _):
                below = pl.ds(pl.multiple_of(j * NB, NB), NB)
                l_ref[below, here] = w[below, here]
                return 0

            lax.fori_loop(k + 1, steps, keep, 0)
        for i in range(1, len(ticks), 2):
            if ticks[i] is not None:
                pl.when(k == i // 2)(ticks[i])

        def update(j, _):
            there = pl.ds(pl.multiple_of(j * CUT, CUT), CUT)
            w[:, there] -= dot16(left[...], right[there, :], NT)
            return 0

        lax.fori_loop((k + 1) * NB // CUT, width // CUT, update, 0)
        return 0

    lax.fori_loop(0, steps, step, 0)


def split_upper(w, m_ref):
    width = w.shape[0]
    for n in range(width // NB):
        cut = slice(n * NB, (n + 1) * NB)
        end = (n + 1) * NB
        hi, lo = split(w[:end, cut])
        m_ref[0, :end, cut] = hi
        m_ref[1, :end, cut] = lo
        if end < width:
            m_ref[:, end:, cut] = jnp.zeros((2, width - end, NB), BF16)


def apply_upper(rows, m_ref, cut):
    return dot16(rows, m_ref[0, : cut.stop, cut]) + dot16(rows, m_ref[1, : cut.stop, cut])


def front_kernel(
    a_ref, keep_ref, raw, parent,
    m_ref, m_pivot, l_ref, g_ref, d_ref, st_ref, lead_out, far_out,
    w, inv_s, up_s, left, right, u_ref, e_ref, lead, m_far, piece, e_y, e_z, st_a,
    send_sems, recv_sems, local_sems,
):
    width = a_ref.shape[0]
    mv, early, swap, pivot_here, late, last = gather_program(
        raw, parent, g_ref, d_ref, st_ref, m_ref, u_ref, e_ref, lead, m_far, piece, e_y, e_z,
        st_a, (send_sems, recv_sems, local_sems),
    )
    cuts = [slice(n, n + CUT) for n in range(0, width, CUT)]
    w[...] = a_ref[...]
    factor_loop(w, inv_s, up_s, left, right, None, early)
    split_upper(w, m_ref)
    mine = pl.ds(pl.multiple_of(mv.core * 512 + mv.at["x"] * 128 + mv.at["z"] * 32, 32), 32)
    for cut in cuts:
        both = apply_upper(u_ref[mine, : cut.stop], m_ref, cut)
        piece[:, cut] = (both * keep_ref[mine, :1]).astype(BF16)
    swap[0]()
    for cut in cuts:
        both = apply_upper(u_ref[:width, : cut.stop], m_ref, cut)
        lead[0, :, cut] = (both * keep_ref[:, :1]).astype(BF16)
    swap[1]()
    pivot_here()

    def subtract(i, cut, total):
        w[cut.start :, cut] = total - dot16(lead[i, cut.start :, :], lead[i, cut, :], NT)

    for n, cut in enumerate(cuts):
        if n == 1:
            swap[2]()
        subtract(0, cut, e_ref[cut.start :, cut].astype(F32))
    for step in swap[3:]:
        step()
    lead_copy = pltpu.make_async_copy(lead, lead_out, local_sems.at[14])
    far_copy = pltpu.make_async_copy(m_far, far_out, local_sems.at[15])
    lead_copy.start()
    for cut in cuts:
        subtract(1, cut, w[cut.start :, cut])
    factor_loop(w, inv_s, up_s, left, right, l_ref, late)
    split_upper(w, m_pivot)
    for step in last[:2]:
        step()
    far_copy.start()
    for step in last[2:]:
        step()
    mv.finish()
    lead_copy.wait()
    far_copy.wait()


def front(block, keep, raw, parent):
    width = block.shape[0]
    chunk = raw.shape[0]
    hbm = pl.BlockSpec(memory_space=pl.ANY)
    vmem = pl.BlockSpec(memory_space=VM)
    pair = jax.ShapeDtypeStruct((2, width, width), BF16)
    return pl.pallas_call(
        front_kernel,
        out_shape=[
            pair,
            pair,
            jax.ShapeDtypeStruct((width, width), F32),
            jax.ShapeDtypeStruct((2, 4, 2, 2, 4, chunk, width), BF16),
            jax.ShapeDtypeStruct((width, width), BF16),
            jax.ShapeDtypeStruct(parent.shape, BF16),
            pair,
            pair,
        ],
        in_specs=[vmem, vmem, hbm, hbm],
        out_specs=[vmem, vmem, vmem, hbm, hbm, hbm, hbm, hbm],
        scratch_shapes=[
            VM((width, width), F32),
            VM((NB, NB), F32),
            VM((NB, NB), F32),
            VM((width, 3 * NB), BF16),
            VM((width, 3 * NB), BF16),
            VM((16 * chunk, width), BF16),
            VM((width, width), BF16),
            VM((2, width, width), BF16),
            VM((2, width, width), BF16),
            VM((32, width), BF16),
            VM((256, width), BF16),
            VM((64, width), BF16),
            VM((2, 256, width), BF16),
            pltpu.SemaphoreType.DMA((LINKS,)),
            pltpu.SemaphoreType.DMA((LINKS,)),
            pltpu.SemaphoreType.DMA((16,)),
        ],
        compiler_params=pltpu.CompilerParams(
            vmem_limit_bytes=52 * 2**20, collective_id=0, has_side_effects=True
        ),
        cost_estimate=pl.CostEstimate(
            flops=120_000_000_000, bytes_accessed=16 * width * width, transcendentals=0
        ),
        name="front",
    )(block, keep, raw, parent)


def chunk_span(chunk):
    return -(-(TB + chunk - 16) // chunk)


def finish_kernel(
    chunk, across, tile_ref, have_ref, flag_ref, gathered, own_hbm, far_hbm, lead_hbm, pivot_hbm,
    l_ref, d_ref, st_ref, parent_ref, out_ref,
    buf, sem, own, far, lead, pivot, load_sem, s_tile, b_tile, s_keep, f_keep,
):
    t = pl.program_id(0)
    tiles = pl.num_programs(0)
    width = b_tile.shape[1]
    span = chunk_span(chunk)
    slot = lax.rem(t, 2)

    def copies(t, slot):
        out = []
        for g in range(2):
            first = tile_ref[g * tiles + t] * TB // chunk
            for i in range(span):
                c = jnp.minimum(first + i, gathered.shape[1] - 1)
                out.append(
                    pltpu.make_async_copy(
                        gathered.at[g ^ flag_ref[2], c],
                        buf.at[slot, g, pl.ds(i * chunk, chunk)],
                        sem.at[slot, g, i],
                    )
                )
        return out

    loads = [
        pltpu.make_async_copy(src, dst, load_sem.at[i])
        for i, (src, dst) in enumerate(
            ((own_hbm, own), (lead_hbm, lead), (far_hbm, far), (pivot_hbm, pivot))
        )
    ]

    @pl.when(t == 0)
    def _():
        for c in copies(t, slot):
            c.start()
        for c in loads:
            c.start()

    @pl.when(t + 1 < tiles)
    def _():
        for c in copies(t + 1, 1 - slot):
            c.start()

    for c in copies(t, slot):
        c.wait()

    @pl.when(t < across)
    def _():
        b_tile[...] = d_ref[...].astype(F32).T

    @pl.when(t >= across)
    def _():
        b_tile[...] = st_ref[...].astype(F32)

    for g, m_ref in enumerate((own, far)):
        have = have_ref[g * tiles + t] != 0
        side = slice(g * width, (g + 1) * width)

        @pl.when(t == 0)
        def _():
            loads[2 * g].wait()
            if g == 0:
                loads[1].wait()

        @pl.when(jnp.logical_not(have))
        def _():
            s_tile[:, side] = jnp.zeros((TB, width), BF16)

        @pl.when(have)
        def _():
            off = pl.multiple_of(lax.rem(tile_ref[g * tiles + t] * TB, chunk), 16)
            for n in range(0, width, WIDE):
                cut = slice(n, n + WIDE)
                rows = buf[slot, g, pl.ds(off, TB), : n + WIDE]
                s_tile[:, g * width + n : g * width + n + WIDE] = apply_upper(
                    rows, m_ref, cut
                ).astype(BF16)
            b_tile[...] -= dot16(s_tile[:, side], lead[g], NT)

    @pl.when(t == 0)
    def _():
        loads[3].wait()

    b_hi, b_lo = split(b_tile[...])

    def panel(n):
        end = n + WIDE
        hi, lo = pivot[0, :end, n:end], pivot[1, :end, n:end]
        return dot16(b_hi[:, :end], hi) + dot16(b_hi[:, :end], lo) + dot16(b_lo[:, :end], hi)

    first = flag_ref[0] != 0
    lead_tile = (flag_ref[1] != 0) & (t < across + width // TB)
    below = t >= across

    @pl.when(jnp.logical_not(below))
    def _():
        here = pl.ds(pl.multiple_of(t * TB, TB), TB)
        s_keep[here, :] = s_tile[...]
        for n in range(0, width, WIDE):
            f_keep[here, n : n + WIDE] = panel(n).astype(BF16)

    @pl.when(below & first & lead_tile)
    def _():
        out_ref[...] = l_ref[...]

    @pl.when(below & first & jnp.logical_not(lead_tile))
    def _():
        for n in range(0, width, WIDE):
            out_ref[:, n : n + WIDE] = panel(n)

    @pl.when(below & jnp.logical_not(first) & lead_tile)
    def _():
        out_ref[...] = jnp.zeros_like(out_ref)

    @pl.when(below & jnp.logical_not(first) & jnp.logical_not(lead_tile))
    def _():
        f = jnp.concatenate([panel(n).astype(BF16) for n in range(0, width, WIDE)], axis=1)
        out_ref[...] = parent_ref[...].astype(F32) - (
            dot16(s_tile[...], s_keep[...], NT) + dot16(f, f_keep[...], NT)
        )


def finish(tiles, have, flags, gathered, m_own, m_far, lead_both, m_pivot, factor, panel, stripe, parent):
    chunk = gathered.shape[2]
    width = lead_both.shape[-1]
    cols = parent.shape[1]
    across = cols // TB
    lead = width // TB
    grid = across + parent.shape[0] // TB
    hbm = pl.BlockSpec(memory_space=pl.ANY)
    pair = VM((2, width, width), BF16)
    stripe_at = lambda t, *_: (jnp.maximum(t - across, 0), 0)
    return pl.pallas_call(
        functools.partial(finish_kernel, chunk, across),
        grid_spec=pltpu.PrefetchScalarGridSpec(
            num_scalar_prefetch=3,
            grid=(grid,),
            in_specs=[
                hbm,
                hbm,
                hbm,
                hbm,
                hbm,
                pl.BlockSpec((TB, width), lambda t, *_: (jnp.clip(t - across, 0, lead - 1), 0)),
                pl.BlockSpec((width, TB), lambda t, *_: (0, jnp.minimum(t, across - 1))),
                pl.BlockSpec((TB, width), stripe_at),
                pl.BlockSpec((TB, cols), stripe_at),
            ],
            out_specs=pl.BlockSpec((TB, cols), stripe_at),
            scratch_shapes=[
                VM((2, 2, chunk_span(chunk) * chunk, width), BF16),
                pltpu.SemaphoreType.DMA((2, 2, chunk_span(chunk))),
                pair,
                pair,
                pair,
                pair,
                pltpu.SemaphoreType.DMA((4,)),
                VM((TB, 2 * width), BF16),
                VM((TB, width), F32),
                VM((cols, 2 * width), BF16),
                VM((cols, width), BF16),
            ],
        ),
        out_shape=jax.ShapeDtypeStruct(parent.shape, F32),
        compiler_params=pltpu.CompilerParams(vmem_limit_bytes=56 * 2**20),
        cost_estimate=pl.CostEstimate(
            flops=60_000_000_000, bytes_accessed=60 * 2**20, transcendentals=0
        ),
        name="finish",
    )(tiles, have, flags, gathered, m_own, m_far, lead_both, m_pivot, factor, panel, stripe, parent)


def locate(tile_map, parent_tiles):
    matches = tile_map[:, None] == jnp.arange(parent_tiles, dtype=jnp.int32)[None, :]
    positions = jnp.arange(tile_map.shape[0], dtype=jnp.int32)[:, None]
    return jnp.sum(jnp.where(matches, positions, 0), axis=0), jnp.any(matches, axis=0)


def per_device(child_update, child_pivot, child_map, parent_front):
    width = child_pivot.shape[-1]
    stripe_rows, block_cols = parent_front.shape
    row_tiles = stripe_rows // TB
    col_tiles = block_cols // TB
    parent_tiles = row_tiles * lax.axis_size("row")
    row = lax.axis_index("row")
    block = lax.axis_index(("grp", "col"))
    raw = child_update[0]
    chunk = raw.shape[0]

    grp = lax.axis_index("grp")
    own_map = jnp.where(grp == 0, child_map, child_map[::-1])
    lead_tiles = jnp.arange(width // TB, dtype=jnp.int32)
    keep = (own_map[0, : width // TB] == lead_tiles).astype(F32)
    keep = jnp.broadcast_to(jnp.repeat(keep, TB)[:, None], (width, 128))
    m_own, m_pivot, pivot_factor, gathered, column_panel, stripe, lead_both, m_far = front(
        child_pivot[0], keep, raw, parent_front
    )
    gathered = gathered.reshape(2, -1, chunk, width)

    wanted_tiles = jnp.concatenate(
        [
            block * col_tiles + jnp.arange(col_tiles, dtype=jnp.int32),
            row * row_tiles + jnp.arange(row_tiles, dtype=jnp.int32),
        ]
    )
    tiles, have = [], []
    for g in range(2):
        inverse, present = locate(own_map[g], parent_tiles)
        tiles.append(inverse[wanted_tiles])
        have.append(present[wanted_tiles].astype(jnp.int32))
    tiles, have = jnp.concatenate(tiles), jnp.concatenate(have)
    flags = jnp.stack([block == 0, row == 0, grp == 1]).astype(jnp.int32)
    return finish(
        tiles, have, flags, gathered, m_own, m_far, lead_both, m_pivot, pivot_factor,
        column_panel, stripe, parent_front,
    )


def solution(mesh):
    in_specs = (P("grp", ("row", "col"), None), P("grp", None, None), P(), P("row", ("grp", "col")))
    out_specs = P("row", ("grp", "col"))
    return jax.shard_map(
        per_device, mesh=mesh, in_specs=in_specs, out_specs=out_specs, check_vma=False
    )
```
